256 devices in a mesh: lend: 32 (over z, x), tp: 8 (over y, core).
Axes of the slice: x: 4, y: 4, z: 8, core: 2. Of those that a mesh axis runs over, the one named last changes fastest.
Arguments:
- queries: bfloat16 [512, 8, 64, 128], P(('lend', 'tp')), may hold values from -8 to 8
- new_keys: bfloat16 [512, 8, 4, 128], P(('lend', 'tp')), may hold values from -12 to 12
- new_values: bfloat16 [512, 8, 4, 128], P(('lend', 'tp')), may hold values from -6 to 6
- home_keys: bfloat16 [512, 512, 8, 128], P('lend', None, 'tp'), may hold values from -8 to 8
- home_values: bfloat16 [512, 512, 8, 128], P('lend', None, 'tp'), may hold values from -6 to 6
- lent_keys: bfloat16 [1024, 512, 8, 128], P('lend', None, 'tp'), may hold values from -8 to 8
- lent_values: bfloat16 [1024, 512, 8, 128], P('lend', None, 'tp'), may hold values from -6 to 6
- lengths: int32 [512], replicated, may hold values from 1 to 32256, as said below
- slot_owner: int32 [1024], replicated, may hold values from -1 to 511, as said below
Outputs:
- attended: bfloat16 [512, 8, 64, 128], P(('lend', 'tp'))
The draws below stay inside these ranges and needn't reach their ends.
Inputs may be any that keep to these rules, and one draw needn't show every extreme that they name: `lengths`: request r belongs to home group r // 16. Of its L cached tokens it holds the first min(L, 512) at home; when L > 512 it has exactly ceil((L - 512) / 512) lent blocks in slot_owner, else none. `slot_owner`: slot s lies on lender s // 32. A request's blocks are numbered from 0 in slot order. No block lies on the lender of its request's own home group. On one lender at most 2 slots hold blocks of one home group's requests, and in every draw some lenders hold exactly 2 for some home group.
All inputs are finite; a program needn't handle non-finite values.
Results may differ from the reference program's by a relative error of at most 0.0031.
Values may be sent and summed in bfloat16 or wider, within the bound.
No kernel may reach another device: no remote copies, remote signals or barrier semaphores. Data moves between devices by JAX's collectives and lax.ppermute only.
A program may use at most 64 MiB of HBM per device.

```python
import math
import jax
import jax.numpy as jnp
from jax import lax

KV_HEADS = 8
HEAD_DIM = 128
STEPS = 4
CAP = 2
HOME_CAP = 512
BLOCK = 512
REQ_DEV = 16
QROWS = 64
GROUPS = 16
SLOT_TOTAL = 1024
REQUESTS = 512
N_LEND = 32


def lender_offsets(lender_key, lender):
    order = jax.random.permutation(lender_key, N_LEND - 1)
    target = N_LEND - 2 - lender
    index_row = jnp.arange(N_LEND - 1)
    swapped = jnp.where(order == target, order[0], jnp.where(index_row == 0, target, order))
    return jnp.where(lender < N_LEND - 1, swapped, order)


def lend_table(key):
    first, second, third, fourth = jax.random.split(key, 4)
    lender_keys = jax.random.split(first, N_LEND)
    lender_ids = jnp.arange(N_LEND)
    offsets = jax.vmap(lender_offsets)(lender_keys, lender_ids)[:, :GROUPS] + 1
    homes = (lender_ids[:, None] + offsets) % N_LEND
    busy = jax.random.randint(second, (N_LEND, 1, 1), 1, 5)
    filled = jax.random.randint(third, (N_LEND, GROUPS, CAP), 0, 4) < busy
    filled = filled | (jnp.arange(GROUPS)[None, :, None] == 0)
    emptied = (lender_ids[:, None, None] == N_LEND - 1) & (jnp.arange(GROUPS)[None, :, None] == GROUPS - 1) & (jnp.arange(CAP)[None, None, :] == CAP - 1)
    filled = filled & jnp.logical_not(emptied)
    local_index = jax.random.randint(fourth, (N_LEND, GROUPS, CAP), 0, REQ_DEV)
    longest = (lender_ids[:, None, None] < N_LEND - 1) & (jnp.arange(GROUPS)[None, :, None] == 0)
    local_index = jnp.where(longest, REQ_DEV - 1, local_index)
    owners = homes[:, :, None] * REQ_DEV + local_index
    return jnp.where(filled, owners, -1).reshape(-1).astype(jnp.int32)


def drawn_keys(key, count, width):
    shape = (count, width, KV_HEADS, HEAD_DIM)
    result = jnp.clip(jax.random.normal(key, shape, jnp.float32), -6.0, 6.0)
    return result.astype(jnp.bfloat16)


def draw_queries(key, part):
    key = jax.random.fold_in(key, 11)
    first = jax.random.fold_in(key, 0)
    shape = (REQUESTS, KV_HEADS, QROWS, HEAD_DIM)
    result = jnp.clip(jax.random.normal(first, shape, jnp.float32), -6.0, 6.0)
    return result.astype(jnp.bfloat16)


def draw_home_keys(key, part):
    key = jax.random.fold_in(key, 12)
    return drawn_keys(key, REQUESTS, HOME_CAP)


def draw_lent_keys(key, part):
    key = jax.random.fold_in(key, 13)
    return drawn_keys(key, SLOT_TOTAL, BLOCK)


def draw_slot_owner(key, part):
    return lend_table(key)


def draw_lengths(key, part):
    owners = lend_table(key)
    key = jax.random.fold_in(key, 22)
    first, second = jax.random.split(key)
    counts = jnp.sum((owners[None, :] == jnp.arange(REQUESTS)[:, None]).astype(jnp.int32), axis=1)
    tail_count = jax.random.randint(first, (REQUESTS,), 1, BLOCK + 1)
    tail_count = jnp.where(jnp.arange(REQUESTS) == REQUESTS - 1, BLOCK, tail_count)
    short_count = jax.random.randint(second, (REQUESTS,), 1, HOME_CAP + 1)
    return jnp.where(counts > 0, HOME_CAP + (counts - 1) * BLOCK + tail_count, short_count).astype(jnp.int32)


def levels(rng, extent, cuts, smallest, high):
    factor_of = 1.0
    for dim, parts in cuts:
        heights = jax.random.uniform(jax.random.fold_in(jax.random.fold_in(rng, 6), dim), (parts,), jnp.float32, smallest / len(cuts), high / len(cuts))
        factor_of = factor_of * jnp.repeat(jnp.exp(heights), extent[dim] // parts).reshape((-1,) + (1,) * (len(extent) - 1 - dim))
    return factor_of


def normal_values(stream_key, shape, deviation, reach, cuts=(), kind=jnp.bfloat16):
    values = jax.random.normal(stream_key, shape, jnp.float32) * deviation
    if len(cuts) > 0:
        values = levels(stream_key, shape, cuts, -0.22, 0.18) * values
    return jnp.clip(values, min=-reach, max=reach).astype(kind)


def setup_inputs(seed: int = 0) -> dict:
    splits = jax.random.split(jax.random.key(seed), 10)
    return {
        "queries": draw_queries(jax.random.fold_in(splits[9], 71), 0),
        "new_keys": normal_values(splits[1], (REQUESTS, KV_HEADS, STEPS, HEAD_DIM), 2.5, 12.0, ((0, 256),)),
        "new_values": normal_values(splits[2], (REQUESTS, KV_HEADS, STEPS, HEAD_DIM), 1.0, 6.0, ((0, 256),)),
        "home_keys": draw_home_keys(jax.random.fold_in(splits[9], 71), 0),
        "home_values": normal_values(splits[4], (REQUESTS, HOME_CAP, KV_HEADS, HEAD_DIM), 1.0, 6.0, ((0, 32), (2, 8))),
        "lent_keys": draw_lent_keys(jax.random.fold_in(splits[9], 71), 0),
        "lent_values": normal_values(splits[6], (SLOT_TOTAL, BLOCK, KV_HEADS, HEAD_DIM), 1.0, 6.0, ((0, 32), (2, 8))),
        "lengths": draw_lengths(jax.random.fold_in(splits[9], 71), 0),
        "slot_owner": draw_slot_owner(jax.random.fold_in(splits[9], 71), 0),
    }


NEG_BIG = -1e+30

def block_numbers(slot_owner):
    position = jnp.arange(slot_owner.shape[0], dtype=jnp.int32)
    matching = slot_owner[:, None] == slot_owner[None, :]
    earlier = position[None, :] < position[:, None]
    return lax.optimization_barrier(jnp.sum(matching & earlier, axis=1)).astype(jnp.int32)

def reference(queries, new_keys, new_values, home_keys, home_values, lent_keys, lent_values, lengths, slot_owner):
    factor = 1.0 / math.sqrt(HEAD_DIM)
    group_size = QROWS // STEPS
    new_visible = jnp.arange(STEPS)[None, :] <= (jnp.arange(QROWS) // group_size)[:, None]

    def home_one(inputs):
        query_rows, keys_new, values_new, keys_home, values_home, length = inputs
        keys_all = jnp.concatenate([keys_home, jnp.transpose(keys_new, (1, 0, 2))], axis=0)
        values_all = jnp.concatenate([values_home, jnp.transpose(values_new, (1, 0, 2))], axis=0)
        scores = jnp.einsum('kqd,jkd->kqj', query_rows.astype(jnp.float32), keys_all.astype(jnp.float32)) * factor
        home_visible = jnp.arange(HOME_CAP) < jnp.minimum(length, HOME_CAP)
        visible = jnp.concatenate([jnp.broadcast_to(home_visible[None, :], (QROWS, HOME_CAP)), new_visible], axis=1)[None]
        masked = jnp.where(visible, scores, NEG_BIG)
        top_score = lax.optimization_barrier(jnp.max(masked, axis=-1))
        exp_terms = jnp.where(visible, jnp.exp(masked - top_score[..., None]), 0.0)
        row_total = lax.optimization_barrier(jnp.sum(exp_terms, axis=-1))
        weights = lax.optimization_barrier(exp_terms.astype(jnp.bfloat16))
        mixture = jnp.einsum('kqj,jkd->kqd', weights.astype(jnp.float32), values_all.astype(jnp.float32))
        return (mixture / row_total[..., None], top_score + jnp.log(row_total))
    home_out, home_lse = lax.map(home_one, (queries, new_keys, new_values, home_keys, home_values, lengths))
    blocks = block_numbers(slot_owner)

    def merge_slot(state_now, slot_data):
        top_all, total_all, mixed_all = state_now
        owner_id, block_id, keys_slot, values_slot = slot_data
        request = jnp.maximum(owner_id, 0)
        filled = owner_id >= 0
        query_rows = lax.dynamic_index_in_dim(queries, request, 0, keepdims=False)
        length = lax.dynamic_index_in_dim(lengths, request, 0, keepdims=False)
        visible = filled & (HOME_CAP + block_id * BLOCK + jnp.arange(BLOCK) < length)
        scores = jnp.einsum('kqd,jkd->kqj', query_rows.astype(jnp.float32), keys_slot.astype(jnp.float32)) * factor
        masked = jnp.where(visible[None, None], scores, NEG_BIG)
        top_score = lax.optimization_barrier(jnp.max(masked, axis=-1))
        exp_terms = jnp.where(visible[None, None], jnp.exp(masked - top_score[..., None]), 0.0)
        divisor = jnp.where(filled, lax.optimization_barrier(jnp.sum(exp_terms, axis=-1)), 1.0)
        weights = lax.optimization_barrier(exp_terms.astype(jnp.bfloat16))
        lent_out = jnp.einsum('kqj,jkd->kqd', weights.astype(jnp.float32), values_slot.astype(jnp.float32)) / divisor[..., None]
        lent_lse = top_score + jnp.log(divisor)
        old_top = lax.dynamic_index_in_dim(top_all, request, 0, keepdims=False)
        old_total = lax.dynamic_index_in_dim(total_all, request, 0, keepdims=False)
        old_mixed = lax.dynamic_index_in_dim(mixed_all, request, 0, keepdims=False)
        new_top = jnp.where(filled, jnp.maximum(old_top, lent_lse), old_top)
        rescale = jnp.exp(old_top - new_top)
        weight_new = jnp.where(filled, jnp.exp(jnp.where(filled, lent_lse, new_top) - new_top), 0.0)
        new_total = old_total * rescale + weight_new
        new_mixed = old_mixed * rescale[..., None] + weight_new[..., None] * lent_out
        top_all = lax.dynamic_update_index_in_dim(top_all, new_top, request, 0)
        total_all = lax.dynamic_update_index_in_dim(total_all, new_total, request, 0)
        mixed_all = lax.dynamic_update_index_in_dim(mixed_all, new_mixed, request, 0)
        return ((top_all, total_all, mixed_all), None)
    start_state = (home_lse, jnp.ones_like(home_lse), home_out)
    final_state, unused = lax.scan(merge_slot, start_state, (slot_owner, blocks, lent_keys, lent_values))
    top_all, total_all, mixed_all = final_state
    return (mixed_all / total_all[..., None]).astype(jnp.bfloat16)
```

```python
import math

import jax
import jax.numpy as jnp
from jax import lax
from jax.experimental import pallas as pl
from jax.experimental.pallas import tpu as pltpu
from jax.sharding import PartitionSpec as P

STEPS = 4
CAP = 2
HOME_CAP = 512
BLOCK = 512
STAT_ROWS = 8
LANES = 128
LENT_GROUP = 8
HOME_GROUP = 2
MERGE_GROUP = 4
LENT_MIB = 58

NEG_BIG = -1e30
FAR = 1 << 30
LOG2E = math.log2(math.e)

VMEM = pltpu.VMEM
SMEM = pltpu.SMEM
HBM = pltpu.HBM


def spec(space):
    return pl.BlockSpec(memory_space=space)


def nt_dot(left, right):
    return lax.dot_general(
        left, right, (((1,), (1,)), ((), ())), preferred_element_type=jnp.float32
    )


def nn_dot(left, right):
    return lax.dot_general(
        left, right, (((1,), (0,)), ((), ())), preferred_element_type=jnp.float32
    )


def pack_kernel(queries, new_keys, new_values, out, news, sems):
    per_source, heads, rows, _ = queries.shape
    fresh = [
        pltpu.make_async_copy(new_keys, news.at[0], sems.at[0]),
        pltpu.make_async_copy(new_values, news.at[1], sems.at[1]),
    ]
    copies = [
        pltpu.make_async_copy(
            queries.at[part], out.at[:, part * rows : (part + 1) * rows], sems.at[2 + part]
        )
        for part in range(per_source)
    ]
    for copy in fresh + copies:
        copy.start()
    for copy in fresh:
        copy.wait()
    for head in range(heads):
        block = [news[kind, part, head] for kind in range(2) for part in range(per_source)]
        block = jnp.concatenate([array.astype(jnp.float32) for array in block], axis=0)
        out[head, per_source * rows :, :] = block.astype(jnp.bfloat16)
    for copy in copies:
        copy.wait()


def pick_kernel(starts, packed_ref, out_ref, *, rows):
    for place in range(out_ref.shape[0] * CAP):
        lender, rank = divmod(place, CAP)
        start = pl.multiple_of(starts[place], 16)
        out_ref[lender, rank * rows : (rank + 1) * rows, :] = packed_ref[pl.ds(start, rows), :]


def home_kernel(
    info, packed_ref, keys, values, tables, asked, out_ref, lse_ref, stats, *, rows, per_source
):
    sources = packed_ref.shape[0]
    requests = sources * per_source
    new_start = rows * per_source
    new_half = STEPS * per_source
    factor = 1.0 / math.sqrt(packed_ref.shape[-1])

    stats[...] = jnp.zeros_like(stats)
    token = lax.broadcasted_iota(jnp.int32, (rows, new_half), 1)
    step = lax.broadcasted_iota(jnp.int32, (rows, new_half), 0) // (rows // STEPS)
    lane = lax.broadcasted_iota(jnp.int32, stats.shape, 1)

    def some(group, carry):
        chosen = [
            (group * HOME_GROUP + near, part)
            for near in range(HOME_GROUP)
            for part in range(per_source)
        ]
        scores, new_scores, mixed, total = [], [], [], []
        news = []
        for source, part in chosen:
            request = source * per_source + part
            query = packed_ref[source, part * rows : (part + 1) * rows, :]
            block = packed_ref[source, new_start : new_start + 2 * new_half, :].astype(jnp.float32)
            new_keys = block[:new_half].astype(jnp.bfloat16)
            news.append(block[new_half:].astype(jnp.bfloat16))
            length = jnp.minimum(info[request], HOME_CAP)
            raw = nt_dot(query, keys[request])
            position = lax.broadcasted_iota(jnp.int32, raw.shape, 1)
            scores.append(jnp.where(position < length, raw, NEG_BIG))
            seen = (token >= part * STEPS) & (token - part * STEPS <= step)
            seen = seen & (token < (part + 1) * STEPS)
            new_scores.append(jnp.where(seen, nt_dot(query, new_keys), NEG_BIG))
        tops = [
            jnp.maximum(jnp.max(old, axis=1, keepdims=True), jnp.max(new, axis=1, keepdims=True))
            for old, new in zip(scores, new_scores)
        ]
        for near, (source, part) in enumerate(chosen):
            terms = jnp.exp2((scores[near] - tops[near]) * (factor * LOG2E))
            new_terms = jnp.exp2((new_scores[near] - tops[near]) * (factor * LOG2E))
            total.append(
                jnp.sum(terms, axis=1, keepdims=True) + jnp.sum(new_terms, axis=1, keepdims=True)
            )
            mixed.append(
                nn_dot(terms.astype(jnp.bfloat16), values[source * per_source + part])
                + nn_dot(new_terms.astype(jnp.bfloat16), news[near])
            )
        collected = stats[...]
        for near, (source, part) in enumerate(chosen):
            request = source * per_source + part
            out_ref[request] = mixed[near] * (1.0 / total[near])
            collected = jnp.where(
                lane == request, tops[near] * factor + jnp.log(total[near]), collected
            )
        stats[...] = collected
        return carry

    lax.fori_loop(0, sources // HOME_GROUP, some, 0)
    turned = stats[...].T[:requests]
    lse_ref[...] = jnp.concatenate([turned] * CAP, axis=1)


def lent_kernel(
    info,
    query_hbm,
    keys_hbm,
    values_hbm,
    home_lse,
    out_ref,
    queries,
    keys,
    values,
    stats,
    sems,
    *,
    rows,
):
    slots = keys_hbm.shape[0]
    homes = query_hbm.shape[0]
    group = min(LENT_GROUP, slots)
    chunks = slots // group
    factor = 1.0 / math.sqrt(query_hbm.shape[-1])

    def copy(kind, chunk):
        source, target = ((keys_hbm, keys), (values_hbm, values))[kind]
        part = pl.ds(chunk * group, group)
        return pltpu.make_async_copy(source.at[part], target.at[part], sems.at[chunk, kind])

    arrival = pltpu.make_async_copy(query_hbm, queries, sems.at[chunks, 0])
    arrival.start()
    for chunk in range(chunks):
        for kind in range(2):
            copy(kind, chunk).start()
    stats[...] = jnp.zeros_like(stats)
    lane = lax.broadcasted_iota(jnp.int32, (rows, stats.shape[1]), 1)
    arrival.wait()

    def some(chunk, carry):
        for kind in range(2):
            copy(kind, chunk).wait()
        scores, placed, mixed, total = [], [], [], []
        for near in range(group):
            slot = chunk * group + near
            place = info[slot]
            length = info[slots + slot]
            home = lax.div(place, CAP)
            start = pl.multiple_of(lax.rem(place, CAP) * rows, rows)
            raw = nt_dot(queries[home, pl.ds(start, rows), :], keys[slot])
            position = lax.broadcasted_iota(jnp.int32, raw.shape, 1)
            scores.append(jnp.where(position < length, raw, NEG_BIG))
            placed.append((home, start))
        tops = [jnp.max(old, axis=1, keepdims=True) for old in scores]
        for near in range(group):
            terms = jnp.exp2((scores[near] - tops[near]) * (factor * LOG2E))
            total.append(jnp.sum(terms, axis=1, keepdims=True))
            mixed.append(nn_dot(terms.astype(jnp.bfloat16), values[chunk * group + near]))
        for near, (home, start) in enumerate(placed):
            out_ref[home, pl.ds(start, rows), :] = (mixed[near] * (1.0 / total[near])).astype(
                jnp.bfloat16
            )
            stats[pl.ds(start, rows), :] = jnp.where(
                lane == home,
                tops[near] * factor + jnp.log(total[near]),
                stats[pl.ds(start, rows), :],
            )
        return carry

    lax.fori_loop(0, chunks, some, 0)
    turned = stats[...].T[:homes]
    high = turned.astype(jnp.bfloat16).astype(jnp.float32)
    middle = (turned - high).astype(jnp.bfloat16).astype(jnp.float32)
    low = turned - high - middle
    shape = (homes, STAT_ROWS, CAP * rows)
    row = lax.broadcasted_iota(jnp.int32, shape, 1)
    packed = jnp.where(
        row == 0,
        high[:, None, :],
        jnp.where(row == 1, middle[:, None, :], jnp.where(row == 2, low[:, None, :], 0.0)),
    )
    out_ref[:, CAP * rows :, :] = packed.astype(jnp.bfloat16)


def combine_kernel(
    info, picks_wide, back_ref, home_out, home_lse, out_ref, mixed, wide, *, rows
):
    lenders = back_ref.shape[0]
    requests = home_out.shape[0]
    count = out_ref.shape[0]
    per_target = requests // count

    lse = jnp.sum(back_ref[:, CAP * rows :, :].astype(jnp.float32), axis=1)
    owner = picks_wide[...]
    belongs = [owner == request for request in range(requests)]

    def per_request(values, reduce, other):
        parts = [
            reduce(jnp.where(mask, values, other), axis=0, keepdims=True) for mask in belongs
        ]
        return jnp.concatenate(parts, axis=0)

    def per_place(values, other):
        result = jnp.full(owner.shape, other, jnp.float32)
        for request, mask in enumerate(belongs):
            result = jnp.where(mask, values[request : request + 1], result)
        return result

    local = home_lse[...]
    tops = per_request(lse, jnp.max, NEG_BIG)
    tops = jnp.maximum(jnp.maximum(tops, pltpu.roll(tops, rows, 1)), local)
    weights = jnp.where(owner >= 0, jnp.exp(lse - per_place(tops, 0.0)), 0.0)
    sums = per_request(weights, jnp.sum, 0.0)
    home_weights = jnp.exp(local - tops)
    inverse = 1.0 / (home_weights + sums + pltpu.roll(sums, rows, 1))
    weights = weights * per_place(inverse, 1.0)
    home_weights = home_weights * inverse
    turned = weights.T
    for lender in range(lenders):
        wide[lender] = jnp.broadcast_to(turned[:, lender : lender + 1], wide.shape[1:])
    home_turned = home_weights.T

    for request in range(requests):
        mixed[request] = home_out[request] * home_turned[:rows, request : request + 1]
    filled = info[0]
    places = lenders * CAP

    def some(step, carry):
        terms = []
        for near in range(MERGE_GROUP):
            entry = step * MERGE_GROUP + near
            index = jnp.minimum(entry, filled - 1)
            place = info[1 + index]
            lender = lax.div(place, CAP)
            part = pl.ds(pl.multiple_of(lax.rem(place, CAP) * rows, rows), rows)
            term = wide[lender, part, :] * back_ref[lender, part, :].astype(jnp.float32)
            terms.append((info[1 + places + index], jnp.where(entry < filled, term, 0.0)))
        for request, term in terms:
            mixed[request] = mixed[request] + term
        return carry

    lax.fori_loop(0, lax.div(filled + MERGE_GROUP - 1, MERGE_GROUP), some, 0)
    for target in range(count):
        for part in range(per_target):
            out_ref[target, part * rows : (part + 1) * rows, :] = mixed[
                target * per_target + part
            ].astype(jnp.bfloat16)


def listed(present, columns):
    count = present.shape[0]
    index = jnp.arange(count, dtype=jnp.int32)
    before = index[None, :] < index[:, None]
    position = jnp.sum(present[None, :] & before, axis=1, dtype=jnp.int32)
    chosen = present[None, :] & (position[None, :] == index[:, None])
    parts = [jnp.sum(present, dtype=jnp.int32).reshape(1)]
    parts += [jnp.sum(jnp.where(chosen, column[None, :], 0), axis=1) for column in columns]
    return jnp.concatenate(parts)


def shards(
    queries,
    new_keys,
    new_values,
    home_keys,
    home_values,
    lent_keys,
    lent_values,
    lengths,
    slot_owner,
):
    tp_count = lax.axis_size("tp")
    lend_count = lax.axis_size("lend")
    me = lax.axis_index("lend").astype(jnp.int32)
    per_source, heads, rows, dim = queries.shape
    requests = per_source * tp_count
    slots = lent_keys.shape[0]
    packed_rows = per_source * (rows + 2 * STEPS)

    def params(mib):
        return pltpu.CompilerParams(vmem_limit_bytes=mib << 20)

    packed = pl.pallas_call(
        pack_kernel,
        out_shape=jax.ShapeDtypeStruct((heads, packed_rows, dim), jnp.bfloat16),
        in_specs=[spec(HBM)] * 3,
        out_specs=spec(VMEM),
        scratch_shapes=[
            pltpu.VMEM((2,) + new_keys.shape, jnp.bfloat16),
            pltpu.SemaphoreType.DMA((2 + per_source,)),
        ],
        compiler_params=params(60),
        name="pack",
    )(queries, new_keys, new_values)
    packed = lax.all_to_all(packed, "tp", split_axis=0, concat_axis=0, tiled=True)

    table = slot_owner.reshape(lend_count, slots)
    local = table - me * requests
    code = jnp.where(
        (local >= 0) & (local < requests),
        jnp.arange(slots, dtype=jnp.int32)[None, :] * requests + local,
        FAR,
    )
    first = jnp.min(code, axis=1)
    second = jnp.min(jnp.where(code > first[:, None], code, FAR), axis=1)
    codes = jnp.stack([first, second], axis=1)
    picks_pair = jnp.where(codes < FAR, codes % requests, -1)
    picks = picks_pair.reshape(-1)
    picks_wide = jnp.repeat(picks_pair, rows, axis=1)

    own = lax.dynamic_slice_in_dim(slot_owner, me * slots, slots)
    slot = jnp.arange(slots, dtype=jnp.int32)
    everywhere = jnp.arange(slot_owner.shape[0], dtype=jnp.int32)
    same = slot_owner[None, :] == own[:, None]
    earlier = everywhere[None, :] < (me * slots + slot)[:, None]
    numbers = jnp.sum(same & earlier, axis=1, dtype=jnp.int32)
    request = jnp.arange(lengths.shape[0], dtype=jnp.int32)
    owner_length = jnp.sum(
        jnp.where(request[None, :] == own[:, None], lengths[None, :], 0), axis=1
    )
    length = owner_length - HOME_CAP - numbers * BLOCK
    home = jnp.where(own >= 0, own // requests, -1)
    before = slot[None, :] < slot[:, None]
    rank = jnp.sum((home[None, :] == home[:, None]) & before, axis=1, dtype=jnp.int32)
    place = jnp.where(own >= 0, home * CAP + rank, me * CAP)
    lent_info = jnp.concatenate([place, jnp.where(own >= 0, length, 0)])
    place_info = listed(
        picks >= 0, [jnp.arange(lend_count * CAP, dtype=jnp.int32), picks]
    )
    home_lengths = lax.dynamic_slice_in_dim(lengths, me * requests, requests)

    starts = jnp.maximum(picks, 0)
    starts = (starts // per_source) * packed_rows + (starts % per_source) * rows
    asked = pl.pallas_call(
        lambda *refs: pick_kernel(*refs, rows=rows),
        out_shape=jax.ShapeDtypeStruct((lend_count, CAP * rows, dim), jnp.bfloat16),
        in_specs=[spec(SMEM), spec(VMEM)],
        out_specs=spec(VMEM),
        compiler_params=params(8),
        name="pick",
    )(starts, packed.reshape(tp_count * packed_rows, dim))
    arrived = lax.all_to_all(asked, "lend", split_axis=0, concat_axis=0, tiled=True)

    home_out, home_lse = pl.pallas_call(
        lambda *refs: home_kernel(*refs, rows=rows, per_source=per_source),
        out_shape=[
            jax.ShapeDtypeStruct((requests, rows, dim), jnp.float32),
            jax.ShapeDtypeStruct((requests, CAP * rows), jnp.float32),
        ],
        in_specs=[spec(SMEM)] + [spec(VMEM)] * 4 + [spec(HBM)],
        out_specs=[spec(VMEM)] * 2,
        scratch_shapes=[pltpu.VMEM((rows, LANES), jnp.float32)],
        compiler_params=params(24),
        cost_estimate=pl.CostEstimate(
            flops=4 * requests * rows * HOME_CAP * dim,
            bytes_accessed=6 << 20,
            transcendentals=requests * rows * HOME_CAP,
        ),
        name="home",
    )(
        home_lengths,
        packed,
        home_keys.reshape(requests, HOME_CAP, dim),
        home_values.reshape(requests, HOME_CAP, dim),
        picks_wide,
        asked,
    )

    back = pl.pallas_call(
        lambda *refs: lent_kernel(*refs, rows=rows),
        out_shape=jax.ShapeDtypeStruct((lend_count, CAP * rows + STAT_ROWS, dim), jnp.bfloat16),
        in_specs=[spec(SMEM)] + [spec(HBM)] * 4,
        out_specs=spec(VMEM),
        scratch_shapes=[
            pltpu.VMEM((lend_count, CAP * rows, dim), jnp.bfloat16),
            pltpu.VMEM((slots, BLOCK, dim), jnp.bfloat16),
            pltpu.VMEM((slots, BLOCK, dim), jnp.bfloat16),
            pltpu.VMEM((CAP * rows, LANES), jnp.float32),
            pltpu.SemaphoreType.DMA((max(slots // LENT_GROUP, 1) + 1, 2)),
        ],
        compiler_params=params(LENT_MIB),
        name="lent",
    )(
        lent_info,
        arrived,
        lent_keys.reshape(slots, BLOCK, dim),
        lent_values.reshape(slots, BLOCK, dim),
        home_lse,
    )
    back = lax.all_to_all(back, "lend", split_axis=0, concat_axis=0, tiled=True)

    attended = pl.pallas_call(
        lambda *refs: combine_kernel(*refs, rows=rows),
        out_shape=jax.ShapeDtypeStruct((tp_count, per_source * rows, dim), jnp.bfloat16),
        in_specs=[spec(SMEM)] + [spec(VMEM)] * 4,
        out_specs=spec(VMEM),
        scratch_shapes=[
            pltpu.VMEM((requests, rows, dim), jnp.float32),
            pltpu.VMEM((lend_count, CAP * rows, LANES), jnp.float32),
        ],
        compiler_params=params(12),
        name="combine",
    )(place_info, picks_wide, back, home_out, home_lse)
    attended = lax.all_to_all(attended, "tp", split_axis=0, concat_axis=0, tiled=True)
    return jnp.swapaxes(attended.reshape(heads, per_source, rows, dim), 0, 1)


def solution(mesh):
    return jax.shard_map(
        shards,
        mesh=mesh,
        in_specs=(
            P(("lend", "tp"), None, None, None),
            P(("lend", "tp"), None, None, None),
            P(("lend", "tp"), None, None, None),
            P("lend", None, "tp", None),
            P("lend", None, "tp", None),
            P("lend", None, "tp", None),
            P("lend", None, "tp", None),
            P(),
            P(),
        ),
        out_specs=P(("lend", "tp"), None, None, None),
        check_vma=False,
    )
```

```python
import math

import jax
import jax.numpy as jnp
from jax import lax
from jax.experimental import pallas as pl
from jax.experimental.pallas import tpu as pltpu
from jax.sharding import PartitionSpec as P

STEPS = 4
CAP = 2
HOME_CAP = 512
BLOCK = 512
STAT_ROWS = 8
LANES = 128
LENT_GROUP = 8
HOME_GROUP = 2
MERGE_GROUP = 4
LENT_MIB = 58

NEG_BIG = -1e30
FAR = 1 << 30
LOG2E = math.log2(math.e)

VMEM = pltpu.VMEM
SMEM = pltpu.SMEM
HBM = pltpu.HBM


def spec(space):
    return pl.BlockSpec(memory_space=space)


def nt_dot(left, right):
    return lax.dot_general(
        left, right, (((1,), (1,)), ((), ())), preferred_element_type=jnp.float32
    )


def nn_dot(left, right):
    return lax.dot_general(
        left, right, (((1,), (0,)), ((), ())), preferred_element_type=jnp.float32
    )


def pack_kernel(queries, new_keys, new_values, out, news, sems):
    per_source, heads, rows, _ = queries.shape
    fresh = [
        pltpu.make_async_copy(new_keys, news.at[0], sems.at[0]),
        pltpu.make_async_copy(new_values, news.at[1], sems.at[1]),
    ]
    copies = [
        pltpu.make_async_copy(
            queries.at[part], out.at[:, part * rows : (part + 1) * rows], sems.at[2 + part]
        )
        for part in range(per_source)
    ]
    for copy in fresh + copies:
        copy.start()
    for copy in fresh:
        copy.wait()
    fresh = [news[kind].astype(jnp.float32) for kind in range(2)]
    for head in range(heads):
        starts = [(part * heads + head) * STEPS for part in range(per_source)]
        block = [array[start : start + STEPS] for array in fresh for start in starts]
        block = jnp.concatenate(block, axis=0)
        out[head, per_source * rows :, :] = block.astype(jnp.bfloat16)
    for copy in copies:
        copy.wait()


def pick_kernel(starts, packed_ref, out_hbm, picked, sems, *, rows):
    lenders = picked.shape[0]
    parts = sems.shape[0]
    size = lenders // parts
    copies = []
    for part in range(parts):
        for place in range(part * size * CAP, (part + 1) * size * CAP):
            lender, rank = divmod(place, CAP)
            start = pl.multiple_of(starts[place], 16)
            picked[lender, rank * rows : (rank + 1) * rows, :] = packed_ref[pl.ds(start, rows), :]
        span = slice(part * size, (part + 1) * size)
        copies.append(pltpu.make_async_copy(picked.at[span], out_hbm.at[span], sems.at[part]))
        copies[-1].start()
    for copy in copies:
        copy.wait()


def home_kernel(
    info, packed_ref, keys, values, tables, asked, out_ref, lse_ref, stats, *, rows, per_source
):
    sources = packed_ref.shape[0]
    requests = sources * per_source
    new_start = rows * per_source
    new_half = STEPS * per_source
    factor = 1.0 / math.sqrt(packed_ref.shape[-1])

    stats[...] = jnp.zeros_like(stats)
    token = lax.broadcasted_iota(jnp.int32, (rows, new_half), 1)
    step = lax.broadcasted_iota(jnp.int32, (rows, new_half), 0) // (rows // STEPS)
    lane = lax.broadcasted_iota(jnp.int32, stats.shape, 1)

    def some(group, carry):
        chosen = [
            (group * HOME_GROUP + near, part)
            for near in range(HOME_GROUP)
            for part in range(per_source)
        ]
        scores, new_scores, mixed, total = [], [], [], []
        news = []
        for source, part in chosen:
            request = source * per_source + part
            query = packed_ref[source, part * rows : (part + 1) * rows, :]
            block = packed_ref[source, new_start : new_start + 2 * new_half, :].astype(jnp.float32)
            new_keys = block[:new_half].astype(jnp.bfloat16)
            news.append(block[new_half:].astype(jnp.bfloat16))
            length = jnp.minimum(info[request], HOME_CAP)
            raw = nt_dot(query, keys[request])
            position = lax.broadcasted_iota(jnp.int32, raw.shape, 1)
            scores.append(jnp.where(position < length, raw, NEG_BIG))
            seen = (token >= part * STEPS) & (token - part * STEPS <= step)
            seen = seen & (token < (part + 1) * STEPS)
            new_scores.append(jnp.where(seen, nt_dot(query, new_keys), NEG_BIG))
        tops = [
            jnp.maximum(jnp.max(old, axis=1, keepdims=True), jnp.max(new, axis=1, keepdims=True))
            for old, new in zip(scores, new_scores)
        ]
        for near, (source, part) in enumerate(chosen):
            terms = jnp.exp2((scores[near] - tops[near]) * (factor * LOG2E))
            new_terms = jnp.exp2((new_scores[near] - tops[near]) * (factor * LOG2E))
            total.append(
                jnp.sum(terms, axis=1, keepdims=True) + jnp.sum(new_terms, axis=1, keepdims=True)
            )
            mixed.append(
                nn_dot(terms.astype(jnp.bfloat16), values[source * per_source + part])
                + nn_dot(new_terms.astype(jnp.bfloat16), news[near])
            )
        collected = stats[...]
        for near, (source, part) in enumerate(chosen):
            request = source * per_source + part
            out_ref[request] = mixed[near] * (1.0 / total[near])
            collected = jnp.where(
                lane == request, tops[near] * factor + jnp.log(total[near]), collected
            )
        stats[...] = collected
        return carry

    lax.fori_loop(0, sources // HOME_GROUP, some, 0)
    turned = stats[...].T[:requests]
    lse_ref[...] = jnp.concatenate([turned] * CAP, axis=1)


def lent_kernel(
    info_hbm,
    query_hbm,
    keys_hbm,
    values_hbm,
    home_lse,
    out_ref,
    info,
    queries,
    keys,
    values,
    stats,
    sems,
    ends,
    *,
    rows,
    chunks,
):
    slots = keys_hbm.shape[0]
    homes = query_hbm.shape[0]
    factor = 1.0 / math.sqrt(query_hbm.shape[-1])

    def copies(chunk):
        first, size = chunks[chunk]
        span = slice(first, first + size)
        return [
            pltpu.make_async_copy(source.at[span], target.at[span], sems.at[chunk, kind])
            for kind, (source, target) in enumerate(((keys_hbm, keys), (values_hbm, values)))
        ]

    arrivals = [
        pltpu.make_async_copy(info_hbm, info, ends.at[0]),
        pltpu.make_async_copy(query_hbm, queries, ends.at[1]),
    ]
    pending = [copies(chunk) for chunk in range(len(chunks))]
    for copy in arrivals + [copy for pair in pending for copy in pair]:
        copy.start()
    stats[...] = jnp.zeros_like(stats)
    lane = lax.broadcasted_iota(jnp.int32, (rows, stats.shape[1]), 1)
    for copy in arrivals:
        copy.wait()

    for (first, size), pair in zip(chunks, pending):
        for copy in pair:
            copy.wait()
        scores, placed, mixed, total = [], [], [], []
        for slot in range(first, first + size):
            place = info[slot]
            length = info[slots + slot]
            home = lax.div(place, CAP)
            start = pl.multiple_of(lax.rem(place, CAP) * rows, rows)
            raw = nt_dot(queries[home, pl.ds(start, rows), :], keys[slot])
            position = lax.broadcasted_iota(jnp.int32, raw.shape, 1)
            scores.append(jnp.where(position < length, raw, NEG_BIG))
            placed.append((home, start))
        tops = [jnp.max(old, axis=1, keepdims=True) for old in scores]
        for near in range(size):
            terms = jnp.exp2((scores[near] - tops[near]) * (factor * LOG2E))
            total.append(jnp.sum(terms, axis=1, keepdims=True))
            mixed.append(nn_dot(terms.astype(jnp.bfloat16), values[first + near]))
        for near, (home, start) in enumerate(placed):
            out_ref[home, pl.ds(start, rows), :] = (mixed[near] * (1.0 / total[near])).astype(
                jnp.bfloat16
            )
            stats[pl.ds(start, rows), :] = jnp.where(
                lane == home,
                tops[near] * factor + jnp.log(total[near]),
                stats[pl.ds(start, rows), :],
            )

    turned = stats[...].T[:homes]
    high = turned.astype(jnp.bfloat16).astype(jnp.float32)
    middle = (turned - high).astype(jnp.bfloat16).astype(jnp.float32)
    low = turned - high - middle
    shape = (homes, STAT_ROWS, CAP * rows)
    row = lax.broadcasted_iota(jnp.int32, shape, 1)
    packed = jnp.where(
        row == 0,
        high[:, None, :],
        jnp.where(row == 1, middle[:, None, :], jnp.where(row == 2, low[:, None, :], 0.0)),
    )
    out_ref[:, CAP * rows :, :] = packed.astype(jnp.bfloat16)


def combine_kernel(
    info_hbm, picks_wide, back_ref, home_out, home_lse, out_ref, info, mixed, wide, sem, *, rows
):
    lenders = back_ref.shape[0]
    requests = home_out.shape[0]
    count = out_ref.shape[0]
    per_target = requests // count
    arrival = pltpu.make_async_copy(info_hbm, info, sem)
    arrival.start()

    lse = jnp.sum(back_ref[:, CAP * rows :, :].astype(jnp.float32), axis=1)
    owner = picks_wide[...]
    belongs = [owner == request for request in range(requests)]

    def per_request(values, reduce, other):
        parts = [
            reduce(jnp.where(mask, values, other), axis=0, keepdims=True) for mask in belongs
        ]
        return jnp.concatenate(parts, axis=0)

    def per_place(values, other):
        result = jnp.full(owner.shape, other, jnp.float32)
        for request, mask in enumerate(belongs):
            result = jnp.where(mask, values[request : request + 1], result)
        return result

    local = home_lse[...]
    tops = per_request(lse, jnp.max, NEG_BIG)
    tops = jnp.maximum(jnp.maximum(tops, pltpu.roll(tops, rows, 1)), local)
    weights = jnp.where(owner >= 0, jnp.exp(lse - per_place(tops, 0.0)), 0.0)
    sums = per_request(weights, jnp.sum, 0.0)
    home_weights = jnp.exp(local - tops)
    inverse = 1.0 / (home_weights + sums + pltpu.roll(sums, rows, 1))
    weights = weights * per_place(inverse, 1.0)
    home_weights = home_weights * inverse
    turned = weights.T
    for lender in range(lenders):
        wide[lender] = jnp.broadcast_to(turned[:, lender : lender + 1], wide.shape[1:])
    home_turned = home_weights.T

    for request in range(requests):
        mixed[request] = home_out[request] * home_turned[:rows, request : request + 1]
    arrival.wait()
    filled = info[0]
    places = lenders * CAP

    def some(step, carry):
        terms = []
        for near in range(MERGE_GROUP):
            entry = step * MERGE_GROUP + near
            index = jnp.minimum(entry, filled - 1)
            place = info[1 + index]
            lender = lax.div(place, CAP)
            part = pl.ds(pl.multiple_of(lax.rem(place, CAP) * rows, rows), rows)
            term = wide[lender, part, :] * back_ref[lender, part, :].astype(jnp.float32)
            terms.append((info[1 + places + index], jnp.where(entry < filled, term, 0.0)))
        for request, term in terms:
            mixed[request] = mixed[request] + term
        return carry

    lax.fori_loop(0, lax.div(filled + MERGE_GROUP - 1, MERGE_GROUP), some, 0)
    for target in range(count):
        for part in range(per_target):
            out_ref[target, part * rows : (part + 1) * rows, :] = mixed[
                target * per_target + part
            ].astype(jnp.bfloat16)


def padded(table):
    return jnp.pad(table, (0, -table.shape[0] % LANES))


def listed(present, columns):
    count = present.shape[0]
    index = jnp.arange(count, dtype=jnp.int32)
    before = index[None, :] < index[:, None]
    position = jnp.sum(present[None, :] & before, axis=1, dtype=jnp.int32)
    chosen = present[None, :] & (position[None, :] == index[:, None])
    parts = [jnp.sum(present, dtype=jnp.int32).reshape(1)]
    parts += [jnp.sum(jnp.where(chosen, column[None, :], 0), axis=1) for column in columns]
    return jnp.concatenate(parts)


def shards(
    queries,
    new_keys,
    new_values,
    home_keys,
    home_values,
    lent_keys,
    lent_values,
    lengths,
    slot_owner,
):
    tp_count = lax.axis_size("tp")
    lend_count = lax.axis_size("lend")
    me = lax.axis_index("lend").astype(jnp.int32)
    per_source, heads, rows, dim = queries.shape
    requests = per_source * tp_count
    slots = lent_keys.shape[0]
    packed_rows = per_source * (rows + 2 * STEPS)

    def params(mib):
        return pltpu.CompilerParams(vmem_limit_bytes=mib << 20)

    packed = pl.pallas_call(
        pack_kernel,
        out_shape=jax.ShapeDtypeStruct((heads, packed_rows, dim), jnp.bfloat16),
        in_specs=[spec(HBM)] * 3,
        out_specs=spec(VMEM),
        scratch_shapes=[
            pltpu.VMEM((2, per_source * heads * STEPS, dim), jnp.bfloat16),
            pltpu.SemaphoreType.DMA((2 + per_source,)),
        ],
        compiler_params=params(60),
        name="pack",
    )(queries, new_keys.reshape(-1, dim), new_values.reshape(-1, dim))
    packed = lax.all_to_all(packed, "tp", split_axis=0, concat_axis=0, tiled=True)

    table = slot_owner.reshape(lend_count, slots)
    local = table - me * requests
    code = jnp.where(
        (local >= 0) & (local < requests),
        jnp.arange(slots, dtype=jnp.int32)[None, :] * requests + local,
        FAR,
    )
    first = jnp.min(code, axis=1)
    second = jnp.min(jnp.where(code > first[:, None], code, FAR), axis=1)
    codes = jnp.stack([first, second], axis=1)
    picks_pair = jnp.where(codes < FAR, codes % requests, -1)
    picks = picks_pair.reshape(-1)
    picks_wide = jnp.repeat(picks_pair, rows, axis=1)

    own = lax.dynamic_slice_in_dim(slot_owner, me * slots, slots)
    slot = jnp.arange(slots, dtype=jnp.int32)
    everywhere = jnp.arange(slot_owner.shape[0], dtype=jnp.int32)
    same = slot_owner[None, :] == own[:, None]
    earlier = everywhere[None, :] < (me * slots + slot)[:, None]
    numbers = jnp.sum(same & earlier, axis=1, dtype=jnp.int32)
    request = jnp.arange(lengths.shape[0], dtype=jnp.int32)
    owner_length = jnp.sum(
        jnp.where(request[None, :] == own[:, None], lengths[None, :], 0), axis=1
    )
    length = owner_length - HOME_CAP - numbers * BLOCK
    home = jnp.where(own >= 0, own // requests, -1)
    before = slot[None, :] < slot[:, None]
    rank = jnp.sum((home[None, :] == home[:, None]) & before, axis=1, dtype=jnp.int32)
    place = jnp.where(own >= 0, home * CAP + rank, me * CAP)
    lent_info = padded(jnp.concatenate([place, jnp.where(own >= 0, length, 0)]))
    place_info = padded(
        listed(picks >= 0, [jnp.arange(lend_count * CAP, dtype=jnp.int32), picks])
    )
    home_lengths = lax.dynamic_slice_in_dim(lengths, me * requests, requests)

    starts = jnp.maximum(picks, 0)
    starts = (starts // per_source) * packed_rows + (starts % per_source) * rows
    asked = pl.pallas_call(
        lambda *refs: pick_kernel(*refs, rows=rows),
        out_shape=jax.ShapeDtypeStruct((lend_count, CAP * rows, dim), jnp.bfloat16),
        in_specs=[spec(SMEM), spec(VMEM)],
        out_specs=spec(HBM),
        scratch_shapes=[
            pltpu.VMEM((lend_count, CAP * rows, dim), jnp.bfloat16),
            pltpu.SemaphoreType.DMA((4,)),
        ],
        compiler_params=params(8),
        name="pick",
    )(starts, packed.reshape(tp_count * packed_rows, dim))
    arrived = lax.all_to_all(asked, "lend", split_axis=0, concat_axis=0, tiled=True)

    home_out, home_lse = pl.pallas_call(
        lambda *refs: home_kernel(*refs, rows=rows, per_source=per_source),
        out_shape=[
            jax.ShapeDtypeStruct((requests, rows, dim), jnp.float32),
            jax.ShapeDtypeStruct((requests, CAP * rows), jnp.float32),
        ],
        in_specs=[spec(SMEM)] + [spec(VMEM)] * 4 + [spec(HBM)],
        out_specs=[spec(VMEM)] * 2,
        scratch_shapes=[pltpu.VMEM((rows, LANES), jnp.float32)],
        compiler_params=params(24),
        cost_estimate=pl.CostEstimate(
            flops=4 * requests * rows * HOME_CAP * dim,
            bytes_accessed=6 << 20,
            transcendentals=requests * rows * HOME_CAP,
        ),
        name="home",
    )(
        home_lengths,
        packed,
        home_keys.reshape(requests, HOME_CAP, dim),
        home_values.reshape(requests, HOME_CAP, dim),
        picks_wide,
        asked,
    )

    sizes = [LENT_GROUP // 2] * 2 + [LENT_GROUP] * (slots // LENT_GROUP - 1)
    chunks = [(sum(sizes[:index]), size) for index, size in enumerate(sizes)]
    back_shape = (lend_count, CAP * rows + STAT_ROWS, dim)
    back = pl.pallas_call(
        lambda *refs: lent_kernel(*refs, rows=rows, chunks=chunks),
        out_shape=jax.ShapeDtypeStruct(back_shape, jnp.bfloat16),
        in_specs=[spec(HBM)] * 5,
        out_specs=spec(VMEM),
        scratch_shapes=[
            pltpu.SMEM(lent_info.shape, jnp.int32),
            pltpu.VMEM((lend_count, CAP * rows, dim), jnp.bfloat16),
            pltpu.VMEM((slots, BLOCK, dim), jnp.bfloat16),
            pltpu.VMEM((slots, BLOCK, dim), jnp.bfloat16),
            pltpu.VMEM((CAP * rows, LANES), jnp.float32),
            pltpu.SemaphoreType.DMA((len(chunks), 2)),
            pltpu.SemaphoreType.DMA((2,)),
        ],
        compiler_params=params(LENT_MIB),
        name="lent",
    )(
        lent_info,
        arrived,
        lent_keys.reshape(slots, BLOCK, dim),
        lent_values.reshape(slots, BLOCK, dim),
        home_lse,
    )
    back = lax.all_to_all(back, "lend", split_axis=0, concat_axis=0, tiled=True)

    attended = pl.pallas_call(
        lambda *refs: combine_kernel(*refs, rows=rows),
        out_shape=jax.ShapeDtypeStruct((tp_count, per_source * rows, dim), jnp.bfloat16),
        in_specs=[spec(HBM)] + [spec(VMEM)] * 4,
        out_specs=spec(VMEM),
        scratch_shapes=[
            pltpu.SMEM(place_info.shape, jnp.int32),
            pltpu.VMEM((requests, rows, dim), jnp.float32),
            pltpu.VMEM((lend_count, CAP * rows, LANES), jnp.float32),
            pltpu.SemaphoreType.DMA,
        ],
        compiler_params=params(12),
        name="combine",
    )(place_info, picks_wide, back, home_out, home_lse)
    attended = lax.all_to_all(attended, "tp", split_axis=0, concat_axis=0, tiled=True)
    return jnp.swapaxes(attended.reshape(heads, per_source, rows, dim), 0, 1)


def solution(mesh):
    return jax.shard_map(
        shards,
        mesh=mesh,
        in_specs=(
            P(("lend", "tp"), None, None, None),
            P(("lend", "tp"), None, None, None),
            P(("lend", "tp"), None, None, None),
            P("lend", None, "tp", None),
            P("lend", None, "tp", None),
            P("lend", None, "tp", None),
            P("lend", None, "tp", None),
            P(),
            P(),
        ),
        out_specs=P(("lend", "tp"), None, None, None),
        check_vma=False,
    )
```

```python
import math

import jax
import jax.numpy as jnp
from jax import lax
from jax.experimental import pallas as pl
from jax.experimental.pallas import tpu as pltpu
from jax.sharding import PartitionSpec as P

STEPS = 4
CAP = 2
HOME_CAP = 512
BLOCK = 512
STAT_ROWS = 8
LANES = 128
LENT_GROUP = 8
HOME_GROUP = 2
MERGE_GROUP = 4
LENT_MIB = 58

NEG_BIG = -1e30
FAR = 1 << 30
LOG2E = math.log2(math.e)

VMEM = pltpu.VMEM
SMEM = pltpu.SMEM
HBM = pltpu.HBM


def spec(space):
    return pl.BlockSpec(memory_space=space)


def nt_dot(left, right):
    return lax.dot_general(
        left, right, (((1,), (1,)), ((), ())), preferred_element_type=jnp.float32
    )


def nn_dot(left, right):
    return lax.dot_general(
        left, right, (((1,), (0,)), ((), ())), preferred_element_type=jnp.float32
    )


def pack_kernel(queries, new_keys, new_values, out, news, sems):
    per_source, heads, rows, _ = queries.shape
    fresh = [
        pltpu.make_async_copy(new_keys, news.at[0], sems.at[0]),
        pltpu.make_async_copy(new_values, news.at[1], sems.at[1]),
    ]
    copies = [
        pltpu.make_async_copy(
            queries.at[part], out.at[:, part * rows : (part + 1) * rows], sems.at[2 + part]
        )
        for part in range(per_source)
    ]
    for copy in fresh + copies:
        copy.start()
    for copy in fresh:
        copy.wait()
    fresh = [news[kind].astype(jnp.float32) for kind in range(2)]
    for head in range(heads):
        starts = [(part * heads + head) * STEPS for part in range(per_source)]
        block = [array[start : start + STEPS] for array in fresh for start in starts]
        block = jnp.concatenate(block, axis=0)
        out[head, per_source * rows :, :] = block.astype(jnp.bfloat16)
    for copy in copies:
        copy.wait()


def pick_kernel(starts, packed_ref, out_hbm, picked, sems, *, rows):
    lenders = picked.shape[0]
    parts = sems.shape[0]
    size = lenders // parts
    copies = []
    for part in range(parts):
        for place in range(part * size * CAP, (part + 1) * size * CAP):
            lender, rank = divmod(place, CAP)
            start = pl.multiple_of(starts[place], 16)
            picked[lender, rank * rows : (rank + 1) * rows, :] = packed_ref[pl.ds(start, rows), :]
        span = slice(part * size, (part + 1) * size)
        copies.append(pltpu.make_async_copy(picked.at[span], out_hbm.at[span], sems.at[part]))
        copies[-1].start()
    for copy in copies:
        copy.wait()


def home_kernel(
    info, packed_ref, keys, values, tables, asked, out_ref, lse_ref, stats, *, rows, per_source
):
    sources = packed_ref.shape[0]
    requests = sources * per_source
    new_start = rows * per_source
    new_half = STEPS * per_source
    factor = 1.0 / math.sqrt(packed_ref.shape[-1])

    stats[...] = jnp.zeros_like(stats)
    token = lax.broadcasted_iota(jnp.int32, (rows, new_half), 1)
    step = lax.broadcasted_iota(jnp.int32, (rows, new_half), 0) // (rows // STEPS)
    lane = lax.broadcasted_iota(jnp.int32, stats.shape, 1)

    def some(group, carry):
        chosen = [
            (group * HOME_GROUP + near, part)
            for near in range(HOME_GROUP)
            for part in range(per_source)
        ]
        scores, new_scores, mixed, total = [], [], [], []
        news = []
        for source, part in chosen:
            request = source * per_source + part
            query = packed_ref[source, part * rows : (part + 1) * rows, :]
            block = packed_ref[source, new_start : new_start + 2 * new_half, :].astype(jnp.float32)
            new_keys = block[:new_half].astype(jnp.bfloat16)
            news.append(block[new_half:].astype(jnp.bfloat16))
            length = jnp.minimum(info[request], HOME_CAP)
            raw = nt_dot(query, keys[request])
            position = lax.broadcasted_iota(jnp.int32, raw.shape, 1)
            scores.append(jnp.where(position < length, raw, NEG_BIG))
            seen = (token >= part * STEPS) & (token - part * STEPS <= step)
            seen = seen & (token < (part + 1) * STEPS)
            new_scores.append(jnp.where(seen, nt_dot(query, new_keys), NEG_BIG))
        tops = [
            jnp.maximum(jnp.max(old, axis=1, keepdims=True), jnp.max(new, axis=1, keepdims=True))
            for old, new in zip(scores, new_scores)
        ]
        for near, (source, part) in enumerate(chosen):
            terms = jnp.exp2((scores[near] - tops[near]) * (factor * LOG2E))
            new_terms = jnp.exp2((new_scores[near] - tops[near]) * (factor * LOG2E))
            total.append(
                jnp.sum(terms, axis=1, keepdims=True) + jnp.sum(new_terms, axis=1, keepdims=True)
            )
            mixed.append(
                nn_dot(terms.astype(jnp.bfloat16), values[source * per_source + part])
                + nn_dot(new_terms.astype(jnp.bfloat16), news[near])
            )
        collected = stats[...]
        for near, (source, part) in enumerate(chosen):
            request = source * per_source + part
            out_ref[request] = mixed[near] * (1.0 / total[near])
            collected = jnp.where(
                lane == request, tops[near] * factor + jnp.log(total[near]), collected
            )
        stats[...] = collected
        return carry

    lax.fori_loop(0, sources // HOME_GROUP, some, 0)
    turned = stats[...].T[:requests]
    lse_ref[...] = jnp.concatenate([turned] * CAP, axis=1)


def lent_kernel(
    info_hbm,
    query_hbm,
    keys_hbm,
    values_hbm,
    home_lse,
    out_ref,
    info,
    queries,
    keys,
    values,
    stats,
    sems,
    ends,
    *,
    rows,
):
    slots = keys_hbm.shape[0]
    homes = query_hbm.shape[0]
    group = min(LENT_GROUP, slots)
    chunks = slots // group
    factor = 1.0 / math.sqrt(query_hbm.shape[-1])

    def copy(kind, chunk):
        source, target = ((keys_hbm, keys), (values_hbm, values))[kind]
        part = pl.ds(chunk * group, group)
        return pltpu.make_async_copy(source.at[part], target.at[part], sems.at[chunk, kind])

    arrivals = [
        pltpu.make_async_copy(info_hbm, info, ends.at[0]),
        pltpu.make_async_copy(query_hbm, queries, ends.at[1]),
    ]
    for arrival in arrivals:
        arrival.start()
    for chunk in range(chunks):
        for kind in range(2):
            copy(kind, chunk).start()
    stats[...] = jnp.zeros_like(stats)
    lane = lax.broadcasted_iota(jnp.int32, (rows, stats.shape[1]), 1)
    for arrival in arrivals:
        arrival.wait()

    def some(chunk, carry):
        for kind in range(2):
            copy(kind, chunk).wait()
        scores, placed, mixed, total = [], [], [], []
        for near in range(group):
            slot = chunk * group + near
            place = info[slot]
            length = info[slots + slot]
            home = lax.div(place, CAP)
            start = pl.multiple_of(lax.rem(place, CAP) * rows, rows)
            raw = nt_dot(queries[home, pl.ds(start, rows), :], keys[slot])
            position = lax.broadcasted_iota(jnp.int32, raw.shape, 1)
            scores.append(jnp.where(position < length, raw, NEG_BIG))
            placed.append((home, start))
        tops = [jnp.max(old, axis=1, keepdims=True) for old in scores]
        for near in range(group):
            terms = jnp.exp2((scores[near] - tops[near]) * (factor * LOG2E))
            total.append(jnp.sum(terms, axis=1, keepdims=True))
            mixed.append(nn_dot(terms.astype(jnp.bfloat16), values[chunk * group + near]))
        for near, (home, start) in enumerate(placed):
            out_ref[home, pl.ds(start, rows), :] = (mixed[near] * (1.0 / total[near])).astype(
                jnp.bfloat16
            )
            stats[pl.ds(start, rows), :] = jnp.where(
                lane == home,
                tops[near] * factor + jnp.log(total[near]),
                stats[pl.ds(start, rows), :],
            )
        return carry

    lax.fori_loop(0, chunks, some, 0)
    turned = stats[...].T[:homes]
    high = turned.astype(jnp.bfloat16).astype(jnp.float32)
    middle = (turned - high).astype(jnp.bfloat16).astype(jnp.float32)
    low = turned - high - middle
    shape = (homes, STAT_ROWS, CAP * rows)
    row = lax.broadcasted_iota(jnp.int32, shape, 1)
    packed = jnp.where(
        row == 0,
        high[:, None, :],
        jnp.where(row == 1, middle[:, None, :], jnp.where(row == 2, low[:, None, :], 0.0)),
    )
    out_ref[:, CAP * rows :, :] = packed.astype(jnp.bfloat16)


def combine_kernel(
    info_hbm, picks_wide, back_ref, home_out, home_lse, out_ref, info, mixed, wide, sem, *, rows
):
    lenders = back_ref.shape[0]
    requests = home_out.shape[0]
    count = out_ref.shape[0]
    per_target = requests // count
    arrival = pltpu.make_async_copy(info_hbm, info, sem)
    arrival.start()

    lse = jnp.sum(back_ref[:, CAP * rows :, :].astype(jnp.float32), axis=1)
    owner = picks_wide[...]
    belongs = [owner == request for request in range(requests)]

    def per_request(values, reduce, other):
        parts = [
            reduce(jnp.where(mask, values, other), axis=0, keepdims=True) for mask in belongs
        ]
        return jnp.concatenate(parts, axis=0)

    def per_place(values, other):
        result = jnp.full(owner.shape, other, jnp.float32)
        for request, mask in enumerate(belongs):
            result = jnp.where(mask, values[request : request + 1], result)
        return result

    local = home_lse[...]
    tops = per_request(lse, jnp.max, NEG_BIG)
    tops = jnp.maximum(jnp.maximum(tops, pltpu.roll(tops, rows, 1)), local)
    weights = jnp.where(owner >= 0, jnp.exp(lse - per_place(tops, 0.0)), 0.0)
    sums = per_request(weights, jnp.sum, 0.0)
    home_weights = jnp.exp(local - tops)
    inverse = 1.0 / (home_weights + sums + pltpu.roll(sums, rows, 1))
    weights = weights * per_place(inverse, 1.0)
    home_weights = home_weights * inverse
    turned = weights.T
    for lender in range(lenders):
        wide[lender] = jnp.broadcast_to(turned[:, lender : lender + 1], wide.shape[1:])
    home_turned = home_weights.T

    for request in range(requests):
        mixed[request] = home_out[request] * home_turned[:rows, request : request + 1]
    arrival.wait()
    filled = info[0]
    places = lenders * CAP

    def some(step, carry):
        terms = []
        for near in range(MERGE_GROUP):
            entry = step * MERGE_GROUP + near
            index = jnp.minimum(entry, filled - 1)
            place = info[1 + index]
            lender = lax.div(place, CAP)
            part = pl.ds(pl.multiple_of(lax.rem(place, CAP) * rows, rows), rows)
            term = wide[lender, part, :] * back_ref[lender, part, :].astype(jnp.float32)
            terms.append((info[1 + places + index], jnp.where(entry < filled, term, 0.0)))
        for request, term in terms:
            mixed[request] = mixed[request] + term
        return carry

    lax.fori_loop(0, lax.div(filled + MERGE_GROUP - 1, MERGE_GROUP), some, 0)
    for target in range(count):
        for part in range(per_target):
            out_ref[target, part * rows : (part + 1) * rows, :] = mixed[
                target * per_target + part
            ].astype(jnp.bfloat16)


def padded(table):
    return jnp.pad(table, (0, -table.shape[0] % LANES))


def listed(present, columns):
    count = present.shape[0]
    index = jnp.arange(count, dtype=jnp.int32)
    before = index[None, :] < index[:, None]
    position = jnp.sum(present[None, :] & before, axis=1, dtype=jnp.int32)
    chosen = present[None, :] & (position[None, :] == index[:, None])
    parts = [jnp.sum(present, dtype=jnp.int32).reshape(1)]
    parts += [jnp.sum(jnp.where(chosen, column[None, :], 0), axis=1) for column in columns]
    return jnp.concatenate(parts)


def shards(
    queries,
    new_keys,
    new_values,
    home_keys,
    home_values,
    lent_keys,
    lent_values,
    lengths,
    slot_owner,
):
    tp_count = lax.axis_size("tp")
    lend_count = lax.axis_size("lend")
    me = lax.axis_index("lend").astype(jnp.int32)
    per_source, heads, rows, dim = queries.shape
    requests = per_source * tp_count
    slots = lent_keys.shape[0]
    packed_rows = per_source * (rows + 2 * STEPS)

    def params(mib):
        return pltpu.CompilerParams(vmem_limit_bytes=mib << 20)

    packed = pl.pallas_call(
        pack_kernel,
        out_shape=jax.ShapeDtypeStruct((heads, packed_rows, dim), jnp.bfloat16),
        in_specs=[spec(HBM)] * 3,
        out_specs=spec(VMEM),
        scratch_shapes=[
            pltpu.VMEM((2, per_source * heads * STEPS, dim), jnp.bfloat16),
            pltpu.SemaphoreType.DMA((2 + per_source,)),
        ],
        compiler_params=params(60),
        name="pack",
    )(queries, new_keys.reshape(-1, dim), new_values.reshape(-1, dim))
    packed = lax.all_to_all(packed, "tp", split_axis=0, concat_axis=0, tiled=True)

    table = slot_owner.reshape(lend_count, slots)
    local = table - me * requests
    code = jnp.where(
        (local >= 0) & (local < requests),
        jnp.arange(slots, dtype=jnp.int32)[None, :] * requests + local,
        FAR,
    )
    first = jnp.min(code, axis=1)
    second = jnp.min(jnp.where(code > first[:, None], code, FAR), axis=1)
    codes = jnp.stack([first, second], axis=1)
    picks_pair = jnp.where(codes < FAR, codes % requests, -1)
    picks = picks_pair.reshape(-1)
    picks_wide = jnp.repeat(picks_pair, rows, axis=1)

    own = lax.dynamic_slice_in_dim(slot_owner, me * slots, slots)
    slot = jnp.arange(slots, dtype=jnp.int32)
    everywhere = jnp.arange(slot_owner.shape[0], dtype=jnp.int32)
    same = slot_owner[None, :] == own[:, None]
    earlier = everywhere[None, :] < (me * slots + slot)[:, None]
    numbers = jnp.sum(same & earlier, axis=1, dtype=jnp.int32)
    request = jnp.arange(lengths.shape[0], dtype=jnp.int32)
    owner_length = jnp.sum(
        jnp.where(request[None, :] == own[:, None], lengths[None, :], 0), axis=1
    )
    length = owner_length - HOME_CAP - numbers * BLOCK
    home = jnp.where(own >= 0, own // requests, -1)
    before = slot[None, :] < slot[:, None]
    rank = jnp.sum((home[None, :] == home[:, None]) & before, axis=1, dtype=jnp.int32)
    place = jnp.where(own >= 0, home * CAP + rank, me * CAP)
    lent_info = padded(jnp.concatenate([place, jnp.where(own >= 0, length, 0)]))
    place_info = padded(
        listed(picks >= 0, [jnp.arange(lend_count * CAP, dtype=jnp.int32), picks])
    )
    home_lengths = lax.dynamic_slice_in_dim(lengths, me * requests, requests)

    starts = jnp.maximum(picks, 0)
    starts = (starts // per_source) * packed_rows + (starts % per_source) * rows
    asked = pl.pallas_call(
        lambda *refs: pick_kernel(*refs, rows=rows),
        out_shape=jax.ShapeDtypeStruct((lend_count, CAP * rows, dim), jnp.bfloat16),
        in_specs=[spec(SMEM), spec(VMEM)],
        out_specs=spec(HBM),
        scratch_shapes=[
            pltpu.VMEM((lend_count, CAP * rows, dim), jnp.bfloat16),
            pltpu.SemaphoreType.DMA((4,)),
        ],
        compiler_params=params(8),
        name="pick",
    )(starts, packed.reshape(tp_count * packed_rows, dim))
    arrived = lax.all_to_all(asked, "lend", split_axis=0, concat_axis=0, tiled=True)

    home_out, home_lse = pl.pallas_call(
        lambda *refs: home_kernel(*refs, rows=rows, per_source=per_source),
        out_shape=[
            jax.ShapeDtypeStruct((requests, rows, dim), jnp.float32),
            jax.ShapeDtypeStruct((requests, CAP * rows), jnp.float32),
        ],
        in_specs=[spec(SMEM)] + [spec(VMEM)] * 4 + [spec(HBM)],
        out_specs=[spec(VMEM)] * 2,
        scratch_shapes=[pltpu.VMEM((rows, LANES), jnp.float32)],
        compiler_params=params(24),
        cost_estimate=pl.CostEstimate(
            flops=4 * requests * rows * HOME_CAP * dim,
            bytes_accessed=6 << 20,
            transcendentals=requests * rows * HOME_CAP,
        ),
        name="home",
    )(
        home_lengths,
        packed,
        home_keys.reshape(requests, HOME_CAP, dim),
        home_values.reshape(requests, HOME_CAP, dim),
        picks_wide,
        asked,
    )

    back_shape = (lend_count, CAP * rows + STAT_ROWS, dim)
    back = pl.pallas_call(
        lambda *refs: lent_kernel(*refs, rows=rows),
        out_shape=jax.ShapeDtypeStruct(back_shape, jnp.bfloat16),
        in_specs=[spec(HBM)] * 5,
        out_specs=spec(VMEM),
        scratch_shapes=[
            pltpu.SMEM(lent_info.shape, jnp.int32),
            pltpu.VMEM((lend_count, CAP * rows, dim), jnp.bfloat16),
            pltpu.VMEM((slots, BLOCK, dim), jnp.bfloat16),
            pltpu.VMEM((slots, BLOCK, dim), jnp.bfloat16),
            pltpu.VMEM((CAP * rows, LANES), jnp.float32),
            pltpu.SemaphoreType.DMA((max(slots // LENT_GROUP, 1), 2)),
            pltpu.SemaphoreType.DMA((2,)),
        ],
        compiler_params=params(LENT_MIB),
        name="lent",
    )(
        lent_info,
        arrived,
        lent_keys.reshape(slots, BLOCK, dim),
        lent_values.reshape(slots, BLOCK, dim),
        home_lse,
    )
    back = lax.all_to_all(back, "lend", split_axis=0, concat_axis=0, tiled=True)

    attended = pl.pallas_call(
        lambda *refs: combine_kernel(*refs, rows=rows),
        out_shape=jax.ShapeDtypeStruct((tp_count, per_source * rows, dim), jnp.bfloat16),
        in_specs=[spec(HBM)] + [spec(VMEM)] * 4,
        out_specs=spec(VMEM),
        scratch_shapes=[
            pltpu.SMEM(place_info.shape, jnp.int32),
            pltpu.VMEM((requests, rows, dim), jnp.float32),
            pltpu.VMEM((lend_count, CAP * rows, LANES), jnp.float32),
            pltpu.SemaphoreType.DMA,
        ],
        compiler_params=params(12),
        name="combine",
    )(place_info, picks_wide, back, home_out, home_lse)
    attended = lax.all_to_all(attended, "tp", split_axis=0, concat_axis=0, tiled=True)
    return jnp.swapaxes(attended.reshape(heads, per_source, rows, dim), 0, 1)


def solution(mesh):
    return jax.shard_map(
        shards,
        mesh=mesh,
        in_specs=(
            P(("lend", "tp"), None, None, None),
            P(("lend", "tp"), None, None, None),
            P(("lend", "tp"), None, None, None),
            P("lend", None, "tp", None),
            P("lend", None, "tp", None),
            P("lend", None, "tp", None),
            P("lend", None, "tp", None),
            P(),
            P(),
        ),
        out_specs=P(("lend", "tp"), None, None, None),
        check_vma=False,
    )
```

```python
import math

import jax
import jax.numpy as jnp
from jax import lax
from jax.experimental import pallas as pl
from jax.experimental.pallas import tpu as pltpu
from jax.sharding import PartitionSpec as P

STEPS = 4
CAP = 2
HOME_CAP = 512
BLOCK = 512
STAT_ROWS = 8
LANES = 128
LENT_GROUP = 8
HOME_GROUP = 2
MERGE_GROUP = 4
LENT_MIB = 58

NEG_BIG = -1e30
FAR = 1 << 30
LOG2E = math.log2(math.e)

VMEM = pltpu.VMEM
SMEM = pltpu.SMEM
HBM = pltpu.HBM


def spec(space):
    return pl.BlockSpec(memory_space=space)


def nt_dot(left, right):
    return lax.dot_general(
        left, right, (((1,), (1,)), ((), ())), preferred_element_type=jnp.float32
    )


def nn_dot(left, right):
    return lax.dot_general(
        left, right, (((1,), (0,)), ((), ())), preferred_element_type=jnp.float32
    )


def pack_kernel(queries, new_keys, new_values, out, news, sems):
    per_source, heads, rows, _ = queries.shape
    fresh = [
        pltpu.make_async_copy(new_keys, news.at[0], sems.at[0]),
        pltpu.make_async_copy(new_values, news.at[1], sems.at[1]),
    ]
    copies = [
        pltpu.make_async_copy(
            queries.at[part], out.at[:, part * rows : (part + 1) * rows], sems.at[2 + part]
        )
        for part in range(per_source)
    ]
    for copy in fresh + copies:
        copy.start()
    for copy in fresh:
        copy.wait()
    fresh = [news[kind].astype(jnp.float32) for kind in range(2)]
    for head in range(heads):
        starts = [(part * heads + head) * STEPS for part in range(per_source)]
        block = [array[start : start + STEPS] for array in fresh for start in starts]
        block = jnp.concatenate(block, axis=0)
        out[head, per_source * rows :, :] = block.astype(jnp.bfloat16)
    for copy in copies:
        copy.wait()


def pick_kernel(starts, packed_ref, out_hbm, picked, sems, *, rows):
    lenders = picked.shape[0]
    parts = sems.shape[0]
    size = lenders // parts
    copies = []
    for part in range(parts):
        for place in range(part * size * CAP, (part + 1) * size * CAP):
            lender, rank = divmod(place, CAP)
            start = pl.multiple_of(starts[place], 16)
            picked[lender, rank * rows : (rank + 1) * rows, :] = packed_ref[pl.ds(start, rows), :]
        span = slice(part * size, (part + 1) * size)
        copies.append(pltpu.make_async_copy(picked.at[span], out_hbm.at[span], sems.at[part]))
        copies[-1].start()
    for copy in copies:
        copy.wait()


def home_kernel(
    info, packed_ref, keys, values, tables, asked, out_ref, lse_ref, stats, *, rows, per_source
):
    sources = packed_ref.shape[0]
    requests = sources * per_source
    new_start = rows * per_source
    new_half = STEPS * per_source
    factor = 1.0 / math.sqrt(packed_ref.shape[-1])

    stats[...] = jnp.zeros_like(stats)
    token = lax.broadcasted_iota(jnp.int32, (rows, new_half), 1)
    step = lax.broadcasted_iota(jnp.int32, (rows, new_half), 0) // (rows // STEPS)
    lane = lax.broadcasted_iota(jnp.int32, stats.shape, 1)

    def some(group, carry):
        chosen = [
            (group * HOME_GROUP + near, part)
            for near in range(HOME_GROUP)
            for part in range(per_source)
        ]
        scores, new_scores, mixed, total = [], [], [], []
        news = []
        for source, part in chosen:
            request = source * per_source + part
            query = packed_ref[source, part * rows : (part + 1) * rows, :]
            block = packed_ref[source, new_start : new_start + 2 * new_half, :].astype(jnp.float32)
            new_keys = block[:new_half].astype(jnp.bfloat16)
            news.append(block[new_half:].astype(jnp.bfloat16))
            length = jnp.minimum(info[request], HOME_CAP)
            raw = nt_dot(query, keys[request])
            position = lax.broadcasted_iota(jnp.int32, raw.shape, 1)
            scores.append(jnp.where(position < length, raw, NEG_BIG))
            seen = (token >= part * STEPS) & (token - part * STEPS <= step)
            seen = seen & (token < (part + 1) * STEPS)
            new_scores.append(jnp.where(seen, nt_dot(query, new_keys), NEG_BIG))
        tops = [
            jnp.maximum(jnp.max(old, axis=1, keepdims=True), jnp.max(new, axis=1, keepdims=True))
            for old, new in zip(scores, new_scores)
        ]
        for near, (source, part) in enumerate(chosen):
            terms = jnp.exp2((scores[near] - tops[near]) * (factor * LOG2E))
            new_terms = jnp.exp2((new_scores[near] - tops[near]) * (factor * LOG2E))
            total.append(
                jnp.sum(terms, axis=1, keepdims=True) + jnp.sum(new_terms, axis=1, keepdims=True)
            )
            mixed.append(
                nn_dot(terms.astype(jnp.bfloat16), values[source * per_source + part])
                + nn_dot(new_terms.astype(jnp.bfloat16), news[near])
            )
        collected = stats[...]
        for near, (source, part) in enumerate(chosen):
            request = source * per_source + part
            out_ref[request] = mixed[near] * (1.0 / total[near])
            collected = jnp.where(
                lane == request, tops[near] * factor + jnp.log(total[near]), collected
            )
        stats[...] = collected
        return carry

    lax.fori_loop(0, sources // HOME_GROUP, some, 0)
    turned = stats[...].T[:requests]
    lse_ref[...] = jnp.concatenate([turned] * CAP, axis=1)


def lent_kernel(
    info,
    query_hbm,
    keys_hbm,
    values_hbm,
    home_lse,
    out_ref,
    queries,
    keys,
    values,
    stats,
    sems,
    *,
    rows,
):
    slots = keys_hbm.shape[0]
    homes = query_hbm.shape[0]
    group = min(LENT_GROUP, slots)
    chunks = slots // group
    factor = 1.0 / math.sqrt(query_hbm.shape[-1])

    def copy(kind, chunk):
        source, target = ((keys_hbm, keys), (values_hbm, values))[kind]
        part = pl.ds(chunk * group, group)
        return pltpu.make_async_copy(source.at[part], target.at[part], sems.at[chunk, kind])

    arrival = pltpu.make_async_copy(query_hbm, queries, sems.at[chunks, 0])
    arrival.start()
    for chunk in range(chunks):
        for kind in range(2):
            copy(kind, chunk).start()
    stats[...] = jnp.zeros_like(stats)
    lane = lax.broadcasted_iota(jnp.int32, (rows, stats.shape[1]), 1)
    position = lax.broadcasted_iota(jnp.int32, (1, BLOCK), 1)
    arrival.wait()

    def some(chunk, carry):
        for kind in range(2):
            copy(kind, chunk).wait()
        scores, placed, mixed, total = [], [], [], []
        for near in range(group):
            slot = chunk * group + near
            place = info[slot]
            length = info[slots + slot]
            home = lax.div(place, CAP)
            first = pl.multiple_of(lax.rem(place, CAP) * rows, rows)
            raw = nt_dot(queries[home, pl.ds(first, rows), :], keys[slot])
            scores.append(raw + jnp.where(position < length, 0.0, NEG_BIG))
            placed.append((home, first))
        tops = [jnp.max(old, axis=1, keepdims=True) for old in scores]
        for near in range(group):
            terms = jnp.exp2((scores[near] - tops[near]) * (factor * LOG2E))
            total.append(jnp.sum(terms, axis=1, keepdims=True))
            mixed.append(nn_dot(terms.astype(jnp.bfloat16), values[chunk * group + near]))
        for near, (home, first) in enumerate(placed):
            out_ref[home, pl.ds(first, rows), :] = (mixed[near] * (1.0 / total[near])).astype(
                jnp.bfloat16
            )
            stats[pl.ds(first, rows), :] = jnp.where(
                lane == home,
                tops[near] * factor + jnp.log(total[near]),
                stats[pl.ds(first, rows), :],
            )
        return carry

    lax.fori_loop(0, chunks, some, 0)
    turned = stats[...].T[:homes]
    high = turned.astype(jnp.bfloat16).astype(jnp.float32)
    middle = (turned - high).astype(jnp.bfloat16).astype(jnp.float32)
    low = turned - high - middle
    shape = (homes, STAT_ROWS, CAP * rows)
    row = lax.broadcasted_iota(jnp.int32, shape, 1)
    packed = jnp.where(
        row == 0,
        high[:, None, :],
        jnp.where(row == 1, middle[:, None, :], jnp.where(row == 2, low[:, None, :], 0.0)),
    )
    out_ref[:, CAP * rows :, :] = packed.astype(jnp.bfloat16)


def combine_kernel(
    info_hbm, picks_wide, back_ref, home_out, home_lse, out_ref, info, mixed, wide, sem, *, rows
):
    lenders = back_ref.shape[0]
    requests = home_out.shape[0]
    count = out_ref.shape[0]
    per_target = requests // count
    arrival = pltpu.make_async_copy(info_hbm, info, sem)
    arrival.start()

    lse = jnp.sum(back_ref[:, CAP * rows :, :].astype(jnp.float32), axis=1)
    owner = picks_wide[...]
    belongs = [owner == request for request in range(requests)]

    def per_request(values, reduce, other):
        parts = [
            reduce(jnp.where(mask, values, other), axis=0, keepdims=True) for mask in belongs
        ]
        return jnp.concatenate(parts, axis=0)

    def per_place(values, other):
        result = jnp.full(owner.shape, other, jnp.float32)
        for request, mask in enumerate(belongs):
            result = jnp.where(mask, values[request : request + 1], result)
        return result

    local = home_lse[...]
    tops = per_request(lse, jnp.max, NEG_BIG)
    tops = jnp.maximum(jnp.maximum(tops, pltpu.roll(tops, rows, 1)), local)
    weights = jnp.where(owner >= 0, jnp.exp(lse - per_place(tops, 0.0)), 0.0)
    sums = per_request(weights, jnp.sum, 0.0)
    home_weights = jnp.exp(local - tops)
    inverse = 1.0 / (home_weights + sums + pltpu.roll(sums, rows, 1))
    weights = weights * per_place(inverse, 1.0)
    home_weights = home_weights * inverse
    turned = weights.T
    for lender in range(lenders):
        wide[lender] = jnp.broadcast_to(turned[:, lender : lender + 1], wide.shape[1:])
    home_turned = home_weights.T

    for request in range(requests):
        mixed[request] = home_out[request] * home_turned[:rows, request : request + 1]
    arrival.wait()
    filled = info[0]
    places = lenders * CAP

    def some(step, carry):
        terms = []
        for near in range(MERGE_GROUP):
            entry = step * MERGE_GROUP + near
            index = jnp.minimum(entry, filled - 1)
            place = info[1 + index]
            lender = lax.div(place, CAP)
            part = pl.ds(pl.multiple_of(lax.rem(place, CAP) * rows, rows), rows)
            term = wide[lender, part, :] * back_ref[lender, part, :].astype(jnp.float32)
            terms.append((info[1 + places + index], jnp.where(entry < filled, term, 0.0)))
        for request, term in terms:
            mixed[request] = mixed[request] + term
        return carry

    lax.fori_loop(0, lax.div(filled + MERGE_GROUP - 1, MERGE_GROUP), some, 0)
    for target in range(count):
        for part in range(per_target):
            out_ref[target, part * rows : (part + 1) * rows, :] = mixed[
                target * per_target + part
            ].astype(jnp.bfloat16)


def padded(table):
    return jnp.pad(table, (0, -table.shape[0] % LANES))


def listed(present, columns):
    count = present.shape[0]
    index = jnp.arange(count, dtype=jnp.int32)
    before = index[None, :] < index[:, None]
    position = jnp.sum(present[None, :] & before, axis=1, dtype=jnp.int32)
    chosen = present[None, :] & (position[None, :] == index[:, None])
    parts = [jnp.sum(present, dtype=jnp.int32).reshape(1)]
    parts += [jnp.sum(jnp.where(chosen, column[None, :], 0), axis=1) for column in columns]
    return jnp.concatenate(parts)


def shards(
    queries,
    new_keys,
    new_values,
    home_keys,
    home_values,
    lent_keys,
    lent_values,
    lengths,
    slot_owner,
):
    tp_count = lax.axis_size("tp")
    lend_count = lax.axis_size("lend")
    me = lax.axis_index("lend").astype(jnp.int32)
    per_source, heads, rows, dim = queries.shape
    requests = per_source * tp_count
    slots = lent_keys.shape[0]
    packed_rows = per_source * (rows + 2 * STEPS)

    def params(mib):
        return pltpu.CompilerParams(vmem_limit_bytes=mib << 20)

    packed = pl.pallas_call(
        pack_kernel,
        out_shape=jax.ShapeDtypeStruct((heads, packed_rows, dim), jnp.bfloat16),
        in_specs=[spec(HBM)] * 3,
        out_specs=spec(VMEM),
        scratch_shapes=[
            pltpu.VMEM((2, per_source * heads * STEPS, dim), jnp.bfloat16),
            pltpu.SemaphoreType.DMA((2 + per_source,)),
        ],
        compiler_params=params(60),
        name="pack",
    )(queries, new_keys.reshape(-1, dim), new_values.reshape(-1, dim))
    packed = lax.all_to_all(packed, "tp", split_axis=0, concat_axis=0, tiled=True)

    table = slot_owner.reshape(lend_count, slots)
    local = table - me * requests
    code = jnp.where(
        (local >= 0) & (local < requests),
        jnp.arange(slots, dtype=jnp.int32)[None, :] * requests + local,
        FAR,
    )
    first = jnp.min(code, axis=1)
    second = jnp.min(jnp.where(code > first[:, None], code, FAR), axis=1)
    codes = jnp.stack([first, second], axis=1)
    picks_pair = jnp.where(codes < FAR, codes % requests, -1)
    picks = picks_pair.reshape(-1)
    picks_wide = jnp.repeat(picks_pair, rows, axis=1)

    own = lax.dynamic_slice_in_dim(slot_owner, me * slots, slots)
    slot = jnp.arange(slots, dtype=jnp.int32)
    everywhere = jnp.arange(slot_owner.shape[0], dtype=jnp.int32)
    same = slot_owner[None, :] == own[:, None]
    earlier = everywhere[None, :] < (me * slots + slot)[:, None]
    numbers = jnp.sum(same & earlier, axis=1, dtype=jnp.int32)
    request = jnp.arange(lengths.shape[0], dtype=jnp.int32)
    owner_length = jnp.sum(
        jnp.where(request[None, :] == own[:, None], lengths[None, :], 0), axis=1
    )
    length = owner_length - HOME_CAP - numbers * BLOCK
    home = jnp.where(own >= 0, own // requests, -1)
    before = slot[None, :] < slot[:, None]
    rank = jnp.sum((home[None, :] == home[:, None]) & before, axis=1, dtype=jnp.int32)
    place = jnp.where(own >= 0, home * CAP + rank, me * CAP)
    lent_info = jnp.concatenate([place, jnp.where(own >= 0, length, 0)])
    place_info = padded(
        listed(picks >= 0, [jnp.arange(lend_count * CAP, dtype=jnp.int32), picks])
    )
    home_lengths = lax.dynamic_slice_in_dim(lengths, me * requests, requests)

    starts = jnp.maximum(picks, 0)
    starts = (starts // per_source) * packed_rows + (starts % per_source) * rows
    asked = pl.pallas_call(
        lambda *refs: pick_kernel(*refs, rows=rows),
        out_shape=jax.ShapeDtypeStruct((lend_count, CAP * rows, dim), jnp.bfloat16),
        in_specs=[spec(SMEM), spec(VMEM)],
        out_specs=spec(HBM),
        scratch_shapes=[
            pltpu.VMEM((lend_count, CAP * rows, dim), jnp.bfloat16),
            pltpu.SemaphoreType.DMA((4,)),
        ],
        compiler_params=params(8),
        name="pick",
    )(starts, packed.reshape(tp_count * packed_rows, dim))
    arrived = lax.all_to_all(asked, "lend", split_axis=0, concat_axis=0, tiled=True)

    home_out, home_lse = pl.pallas_call(
        lambda *refs: home_kernel(*refs, rows=rows, per_source=per_source),
        out_shape=[
            jax.ShapeDtypeStruct((requests, rows, dim), jnp.float32),
            jax.ShapeDtypeStruct((requests, CAP * rows), jnp.float32),
        ],
        in_specs=[spec(SMEM)] + [spec(VMEM)] * 4 + [spec(HBM)],
        out_specs=[spec(VMEM)] * 2,
        scratch_shapes=[pltpu.VMEM((rows, LANES), jnp.float32)],
        compiler_params=params(24),
        cost_estimate=pl.CostEstimate(
            flops=4 * requests * rows * HOME_CAP * dim,
            bytes_accessed=6 << 20,
            transcendentals=requests * rows * HOME_CAP,
        ),
        name="home",
    )(
        home_lengths,
        packed,
        home_keys.reshape(requests, HOME_CAP, dim),
        home_values.reshape(requests, HOME_CAP, dim),
        picks_wide,
        asked,
    )

    back_shape = (lend_count, CAP * rows + STAT_ROWS, dim)
    back = pl.pallas_call(
        lambda *refs: lent_kernel(*refs, rows=rows),
        out_shape=jax.ShapeDtypeStruct(back_shape, jnp.bfloat16),
        in_specs=[spec(SMEM)] + [spec(HBM)] * 4,
        out_specs=spec(VMEM),
        scratch_shapes=[
            pltpu.VMEM((lend_count, CAP * rows, dim), jnp.bfloat16),
            pltpu.VMEM((slots, BLOCK, dim), jnp.bfloat16),
            pltpu.VMEM((slots, BLOCK, dim), jnp.bfloat16),
            pltpu.VMEM((CAP * rows, LANES), jnp.float32),
            pltpu.SemaphoreType.DMA((max(slots // LENT_GROUP, 1) + 1, 2)),
        ],
        compiler_params=params(LENT_MIB),
        name="lent",
    )(
        lent_info,
        arrived,
        lent_keys.reshape(slots, BLOCK, dim),
        lent_values.reshape(slots, BLOCK, dim),
        home_lse,
    )
    back = lax.all_to_all(back, "lend", split_axis=0, concat_axis=0, tiled=True)

    attended = pl.pallas_call(
        lambda *refs: combine_kernel(*refs, rows=rows),
        out_shape=jax.ShapeDtypeStruct((tp_count, per_source * rows, dim), jnp.bfloat16),
        in_specs=[spec(HBM)] + [spec(VMEM)] * 4,
        out_specs=spec(VMEM),
        scratch_shapes=[
            pltpu.SMEM(place_info.shape, jnp.int32),
            pltpu.VMEM((requests, rows, dim), jnp.float32),
            pltpu.VMEM((lend_count, CAP * rows, LANES), jnp.float32),
            pltpu.SemaphoreType.DMA,
        ],
        compiler_params=params(12),
        name="combine",
    )(place_info, picks_wide, back, home_out, home_lse)
    attended = lax.all_to_all(attended, "tp", split_axis=0, concat_axis=0, tiled=True)
    return jnp.swapaxes(attended.reshape(heads, per_source, rows, dim), 0, 1)


def solution(mesh):
    return jax.shard_map(
        shards,
        mesh=mesh,
        in_specs=(
            P(("lend", "tp"), None, None, None),
            P(("lend", "tp"), None, None, None),
            P(("lend", "tp"), None, None, None),
            P("lend", None, "tp", None),
            P("lend", None, "tp", None),
            P("lend", None, "tp", None),
            P("lend", None, "tp", None),
            P(),
            P(),
        ),
        out_specs=P(("lend", "tp"), None, None, None),
        check_vma=False,
    )
```

```python
import math

import jax
import jax.numpy as jnp
from jax import lax
from jax.experimental import pallas as pl
from jax.experimental.pallas import tpu as pltpu
from jax.sharding import PartitionSpec as P

STEPS = 4
CAP = 2
HOME_CAP = 512
BLOCK = 512
STAT_ROWS = 8
LANES = 128
LENT_GROUP = 16
HOME_GROUP = 2
MERGE_GROUP = 4
LENT_MIB = 58

NEG_BIG = -1e30
FAR = 1 << 30
LOG2E = math.log2(math.e)

VMEM = pltpu.VMEM
SMEM = pltpu.SMEM
HBM = pltpu.HBM


def spec(space):
    return pl.BlockSpec(memory_space=space)


def nt_dot(left, right):
    return lax.dot_general(
        left, right, (((1,), (1,)), ((), ())), preferred_element_type=jnp.float32
    )


def nn_dot(left, right):
    return lax.dot_general(
        left, right, (((1,), (0,)), ((), ())), preferred_element_type=jnp.float32
    )


def pack_kernel(queries, new_keys, new_values, out, news, sems):
    per_source, heads, rows, _ = queries.shape
    fresh = [
        pltpu.make_async_copy(new_keys, news.at[0], sems.at[0]),
        pltpu.make_async_copy(new_values, news.at[1], sems.at[1]),
    ]
    copies = [
        pltpu.make_async_copy(
            queries.at[part], out.at[:, part * rows : (part + 1) * rows], sems.at[2 + part]
        )
        for part in range(per_source)
    ]
    for copy in fresh + copies:
        copy.start()
    for copy in fresh:
        copy.wait()
    fresh = [news[kind].astype(jnp.float32) for kind in range(2)]
    for head in range(heads):
        starts = [(part * heads + head) * STEPS for part in range(per_source)]
        block = [array[start : start + STEPS] for array in fresh for start in starts]
        block = jnp.concatenate(block, axis=0)
        out[head, per_source * rows :, :] = block.astype(jnp.bfloat16)
    for copy in copies:
        copy.wait()


def pick_kernel(starts, packed_ref, out_hbm, picked, sems, *, rows):
    lenders = picked.shape[0]
    parts = sems.shape[0]
    size = lenders // parts
    copies = []
    for part in range(parts):
        for place in range(part * size * CAP, (part + 1) * size * CAP):
            lender, rank = divmod(place, CAP)
            start = pl.multiple_of(starts[place], 16)
            picked[lender, rank * rows : (rank + 1) * rows, :] = packed_ref[pl.ds(start, rows), :]
        span = slice(part * size, (part + 1) * size)
        copies.append(pltpu.make_async_copy(picked.at[span], out_hbm.at[span], sems.at[part]))
        copies[-1].start()
    for copy in copies:
        copy.wait()


def home_kernel(
    info, packed_ref, keys, values, tables, asked, out_ref, lse_ref, stats, *, rows, per_source
):
    sources = packed_ref.shape[0]
    requests = sources * per_source
    new_start = rows * per_source
    new_half = STEPS * per_source
    factor = 1.0 / math.sqrt(packed_ref.shape[-1])

    stats[...] = jnp.zeros_like(stats)
    token = lax.broadcasted_iota(jnp.int32, (rows, new_half), 1)
    step = lax.broadcasted_iota(jnp.int32, (rows, new_half), 0) // (rows // STEPS)
    lane = lax.broadcasted_iota(jnp.int32, stats.shape, 1)

    def some(group, carry):
        chosen = [
            (group * HOME_GROUP + near, part)
            for near in range(HOME_GROUP)
            for part in range(per_source)
        ]
        scores, new_scores, mixed, total = [], [], [], []
        news = []
        for source, part in chosen:
            request = source * per_source + part
            query = packed_ref[source, part * rows : (part + 1) * rows, :]
            block = packed_ref[source, new_start : new_start + 2 * new_half, :].astype(jnp.float32)
            new_keys = block[:new_half].astype(jnp.bfloat16)
            news.append(block[new_half:].astype(jnp.bfloat16))
            length = jnp.minimum(info[request], HOME_CAP)
            raw = nt_dot(query, keys[request])
            position = lax.broadcasted_iota(jnp.int32, raw.shape, 1)
            scores.append(jnp.where(position < length, raw, NEG_BIG))
            seen = (token >= part * STEPS) & (token - part * STEPS <= step)
            seen = seen & (token < (part + 1) * STEPS)
            new_scores.append(jnp.where(seen, nt_dot(query, new_keys), NEG_BIG))
        tops = [
            jnp.maximum(jnp.max(old, axis=1, keepdims=True), jnp.max(new, axis=1, keepdims=True))
            for old, new in zip(scores, new_scores)
        ]
        for near, (source, part) in enumerate(chosen):
            terms = jnp.exp2((scores[near] - tops[near]) * (factor * LOG2E))
            new_terms = jnp.exp2((new_scores[near] - tops[near]) * (factor * LOG2E))
            total.append(
                jnp.sum(terms, axis=1, keepdims=True) + jnp.sum(new_terms, axis=1, keepdims=True)
            )
            mixed.append(
                nn_dot(terms.astype(jnp.bfloat16), values[source * per_source + part])
                + nn_dot(new_terms.astype(jnp.bfloat16), news[near])
            )
        collected = stats[...]
        for near, (source, part) in enumerate(chosen):
            request = source * per_source + part
            out_ref[request] = mixed[near] * (1.0 / total[near])
            collected = jnp.where(
                lane == request, tops[near] * factor + jnp.log(total[near]), collected
            )
        stats[...] = collected
        return carry

    lax.fori_loop(0, sources // HOME_GROUP, some, 0)
    turned = stats[...].T[:requests]
    lse_ref[...] = jnp.concatenate([turned] * CAP, axis=1)


def lent_kernel(
    info,
    query_hbm,
    keys_hbm,
    values_hbm,
    home_lse,
    out_ref,
    queries,
    keys,
    values,
    stats,
    sems,
    *,
    rows,
):
    slots = keys_hbm.shape[0]
    homes = query_hbm.shape[0]
    group = min(LENT_GROUP, slots)
    chunks = slots // group
    factor = 1.0 / math.sqrt(query_hbm.shape[-1])

    def copy(kind, chunk):
        source, target = ((keys_hbm, keys), (values_hbm, values))[kind]
        part = pl.ds(chunk * group, group)
        return pltpu.make_async_copy(source.at[part], target.at[part], sems.at[chunk, kind])

    arrival = pltpu.make_async_copy(query_hbm, queries, sems.at[chunks, 0])
    arrival.start()
    for chunk in range(chunks):
        for kind in range(2):
            copy(kind, chunk).start()
    stats[...] = jnp.zeros_like(stats)
    lane = lax.broadcasted_iota(jnp.int32, (rows, stats.shape[1]), 1)
    position = lax.broadcasted_iota(jnp.int32, (1, BLOCK), 1)
    arrival.wait()

    def some(chunk, carry):
        for kind in range(2):
            copy(kind, chunk).wait()
        scores, placed, mixed, total = [], [], [], []
        for near in range(group):
            slot = chunk * group + near
            place = info[slot]
            length = info[slots + slot]
            home = lax.div(place, CAP)
            first = pl.multiple_of(lax.rem(place, CAP) * rows, rows)
            raw = nt_dot(queries[home, pl.ds(first, rows), :], keys[slot])
            scores.append(raw + jnp.where(position < length, 0.0, NEG_BIG))
            placed.append((home, first))
        tops = [jnp.max(old, axis=1, keepdims=True) for old in scores]
        for near in range(group):
            terms = jnp.exp2((scores[near] - tops[near]) * (factor * LOG2E))
            total.append(jnp.sum(terms, axis=1, keepdims=True))
            mixed.append(nn_dot(terms.astype(jnp.bfloat16), values[chunk * group + near]))
        for near, (home, first) in enumerate(placed):
            out_ref[home, pl.ds(first, rows), :] = (mixed[near] * (1.0 / total[near])).astype(
                jnp.bfloat16
            )
            stats[pl.ds(first, rows), :] = jnp.where(
                lane == home,
                tops[near] * factor + jnp.log(total[near]),
                stats[pl.ds(first, rows), :],
            )
        return carry

    lax.fori_loop(0, chunks, some, 0)
    turned = stats[...].T[:homes]
    high = turned.astype(jnp.bfloat16).astype(jnp.float32)
    middle = (turned - high).astype(jnp.bfloat16).astype(jnp.float32)
    low = turned - high - middle
    shape = (homes, STAT_ROWS, CAP * rows)
    row = lax.broadcasted_iota(jnp.int32, shape, 1)
    packed = jnp.where(
        row == 0,
        high[:, None, :],
        jnp.where(row == 1, middle[:, None, :], jnp.where(row == 2, low[:, None, :], 0.0)),
    )
    out_ref[:, CAP * rows :, :] = packed.astype(jnp.bfloat16)


def combine_kernel(
    info_hbm, picks_wide, back_ref, home_out, home_lse, out_ref, info, mixed, wide, sem, *, rows
):
    lenders = back_ref.shape[0]
    requests = home_out.shape[0]
    count = out_ref.shape[0]
    per_target = requests // count
    arrival = pltpu.make_async_copy(info_hbm, info, sem)
    arrival.start()

    lse = jnp.sum(back_ref[:, CAP * rows :, :].astype(jnp.float32), axis=1)
    owner = picks_wide[...]
    belongs = [owner == request for request in range(requests)]

    def per_request(values, reduce, other):
        parts = [
            reduce(jnp.where(mask, values, other), axis=0, keepdims=True) for mask in belongs
        ]
        return jnp.concatenate(parts, axis=0)

    def per_place(values, other):
        result = jnp.full(owner.shape, other, jnp.float32)
        for request, mask in enumerate(belongs):
            result = jnp.where(mask, values[request : request + 1], result)
        return result

    local = home_lse[...]
    tops = per_request(lse, jnp.max, NEG_BIG)
    tops = jnp.maximum(jnp.maximum(tops, pltpu.roll(tops, rows, 1)), local)
    weights = jnp.where(owner >= 0, jnp.exp(lse - per_place(tops, 0.0)), 0.0)
    sums = per_request(weights, jnp.sum, 0.0)
    home_weights = jnp.exp(local - tops)
    inverse = 1.0 / (home_weights + sums + pltpu.roll(sums, rows, 1))
    weights = weights * per_place(inverse, 1.0)
    home_weights = home_weights * inverse
    turned = weights.T
    for lender in range(lenders):
        wide[lender] = jnp.broadcast_to(turned[:, lender : lender + 1], wide.shape[1:])
    home_turned = home_weights.T

    for request in range(requests):
        mixed[request] = home_out[request] * home_turned[:rows, request : request + 1]
    arrival.wait()
    filled = info[0]
    places = lenders * CAP

    def some(step, carry):
        terms = []
        for near in range(MERGE_GROUP):
            entry = step * MERGE_GROUP + near
            index = jnp.minimum(entry, filled - 1)
            place = info[1 + index]
            lender = lax.div(place, CAP)
            part = pl.ds(pl.multiple_of(lax.rem(place, CAP) * rows, rows), rows)
            term = wide[lender, part, :] * back_ref[lender, part, :].astype(jnp.float32)
            terms.append((info[1 + places + index], jnp.where(entry < filled, term, 0.0)))
        for request, term in terms:
            mixed[request] = mixed[request] + term
        return carry

    lax.fori_loop(0, lax.div(filled + MERGE_GROUP - 1, MERGE_GROUP), some, 0)
    for target in range(count):
        for part in range(per_target):
            out_ref[target, part * rows : (part + 1) * rows, :] = mixed[
                target * per_target + part
            ].astype(jnp.bfloat16)


def padded(table):
    return jnp.pad(table, (0, -table.shape[0] % LANES))


def listed(present, columns):
    count = present.shape[0]
    index = jnp.arange(count, dtype=jnp.int32)
    before = index[None, :] < index[:, None]
    position = jnp.sum(present[None, :] & before, axis=1, dtype=jnp.int32)
    chosen = present[None, :] & (position[None, :] == index[:, None])
    parts = [jnp.sum(present, dtype=jnp.int32).reshape(1)]
    parts += [jnp.sum(jnp.where(chosen, column[None, :], 0), axis=1) for column in columns]
    return jnp.concatenate(parts)


def shards(
    queries,
    new_keys,
    new_values,
    home_keys,
    home_values,
    lent_keys,
    lent_values,
    lengths,
    slot_owner,
):
    tp_count = lax.axis_size("tp")
    lend_count = lax.axis_size("lend")
    me = lax.axis_index("lend").astype(jnp.int32)
    per_source, heads, rows, dim = queries.shape
    requests = per_source * tp_count
    slots = lent_keys.shape[0]
    packed_rows = per_source * (rows + 2 * STEPS)

    def params(mib):
        return pltpu.CompilerParams(vmem_limit_bytes=mib << 20)

    packed = pl.pallas_call(
        pack_kernel,
        out_shape=jax.ShapeDtypeStruct((heads, packed_rows, dim), jnp.bfloat16),
        in_specs=[spec(HBM)] * 3,
        out_specs=spec(VMEM),
        scratch_shapes=[
            pltpu.VMEM((2, per_source * heads * STEPS, dim), jnp.bfloat16),
            pltpu.SemaphoreType.DMA((2 + per_source,)),
        ],
        compiler_params=params(60),
        name="pack",
    )(queries, new_keys.reshape(-1, dim), new_values.reshape(-1, dim))
    packed = lax.all_to_all(packed, "tp", split_axis=0, concat_axis=0, tiled=True)

    table = slot_owner.reshape(lend_count, slots)
    local = table - me * requests
    code = jnp.where(
        (local >= 0) & (local < requests),
        jnp.arange(slots, dtype=jnp.int32)[None, :] * requests + local,
        FAR,
    )
    first = jnp.min(code, axis=1)
    second = jnp.min(jnp.where(code > first[:, None], code, FAR), axis=1)
    codes = jnp.stack([first, second], axis=1)
    picks_pair = jnp.where(codes < FAR, codes % requests, -1)
    picks = picks_pair.reshape(-1)
    picks_wide = jnp.repeat(picks_pair, rows, axis=1)

    own = lax.dynamic_slice_in_dim(slot_owner, me * slots, slots)
    slot = jnp.arange(slots, dtype=jnp.int32)
    everywhere = jnp.arange(slot_owner.shape[0], dtype=jnp.int32)
    same = slot_owner[None, :] == own[:, None]
    earlier = everywhere[None, :] < (me * slots + slot)[:, None]
    numbers = jnp.sum(same & earlier, axis=1, dtype=jnp.int32)
    request = jnp.arange(lengths.shape[0], dtype=jnp.int32)
    owner_length = jnp.sum(
        jnp.where(request[None, :] == own[:, None], lengths[None, :], 0), axis=1
    )
    length = owner_length - HOME_CAP - numbers * BLOCK
    home = jnp.where(own >= 0, own // requests, -1)
    before = slot[None, :] < slot[:, None]
    rank = jnp.sum((home[None, :] == home[:, None]) & before, axis=1, dtype=jnp.int32)
    place = jnp.where(own >= 0, home * CAP + rank, me * CAP)
    lent_info = jnp.concatenate([place, jnp.where(own >= 0, length, 0)])
    place_info = padded(
        listed(picks >= 0, [jnp.arange(lend_count * CAP, dtype=jnp.int32), picks])
    )
    home_lengths = lax.dynamic_slice_in_dim(lengths, me * requests, requests)

    starts = jnp.maximum(picks, 0)
    starts = (starts // per_source) * packed_rows + (starts % per_source) * rows
    asked = pl.pallas_call(
        lambda *refs: pick_kernel(*refs, rows=rows),
        out_shape=jax.ShapeDtypeStruct((lend_count, CAP * rows, dim), jnp.bfloat16),
        in_specs=[spec(SMEM), spec(VMEM)],
        out_specs=spec(HBM),
        scratch_shapes=[
            pltpu.VMEM((lend_count, CAP * rows, dim), jnp.bfloat16),
            pltpu.SemaphoreType.DMA((4,)),
        ],
        compiler_params=params(8),
        name="pick",
    )(starts, packed.reshape(tp_count * packed_rows, dim))
    arrived = lax.all_to_all(asked, "lend", split_axis=0, concat_axis=0, tiled=True)

    home_out, home_lse = pl.pallas_call(
        lambda *refs: home_kernel(*refs, rows=rows, per_source=per_source),
        out_shape=[
            jax.ShapeDtypeStruct((requests, rows, dim), jnp.float32),
            jax.ShapeDtypeStruct((requests, CAP * rows), jnp.float32),
        ],
        in_specs=[spec(SMEM)] + [spec(VMEM)] * 4 + [spec(HBM)],
        out_specs=[spec(VMEM)] * 2,
        scratch_shapes=[pltpu.VMEM((rows, LANES), jnp.float32)],
        compiler_params=params(24),
        cost_estimate=pl.CostEstimate(
            flops=4 * requests * rows * HOME_CAP * dim,
            bytes_accessed=6 << 20,
            transcendentals=requests * rows * HOME_CAP,
        ),
        name="home",
    )(
        home_lengths,
        packed,
        home_keys.reshape(requests, HOME_CAP, dim),
        home_values.reshape(requests, HOME_CAP, dim),
        picks_wide,
        asked,
    )

    back_shape = (lend_count, CAP * rows + STAT_ROWS, dim)
    back = pl.pallas_call(
        lambda *refs: lent_kernel(*refs, rows=rows),
        out_shape=jax.ShapeDtypeStruct(back_shape, jnp.bfloat16),
        in_specs=[spec(SMEM)] + [spec(HBM)] * 4,
        out_specs=spec(VMEM),
        scratch_shapes=[
            pltpu.VMEM((lend_count, CAP * rows, dim), jnp.bfloat16),
            pltpu.VMEM((slots, BLOCK, dim), jnp.bfloat16),
            pltpu.VMEM((slots, BLOCK, dim), jnp.bfloat16),
            pltpu.VMEM((CAP * rows, LANES), jnp.float32),
            pltpu.SemaphoreType.DMA((max(slots // LENT_GROUP, 1) + 1, 2)),
        ],
        compiler_params=params(LENT_MIB),
        name="lent",
    )(
        lent_info,
        arrived,
        lent_keys.reshape(slots, BLOCK, dim),
        lent_values.reshape(slots, BLOCK, dim),
        home_lse,
    )
    back = lax.all_to_all(back, "lend", split_axis=0, concat_axis=0, tiled=True)

    attended = pl.pallas_call(
        lambda *refs: combine_kernel(*refs, rows=rows),
        out_shape=jax.ShapeDtypeStruct((tp_count, per_source * rows, dim), jnp.bfloat16),
        in_specs=[spec(HBM)] + [spec(VMEM)] * 4,
        out_specs=spec(VMEM),
        scratch_shapes=[
            pltpu.SMEM(place_info.shape, jnp.int32),
            pltpu.VMEM((requests, rows, dim), jnp.float32),
            pltpu.VMEM((lend_count, CAP * rows, LANES), jnp.float32),
            pltpu.SemaphoreType.DMA,
        ],
        compiler_params=params(12),
        name="combine",
    )(place_info, picks_wide, back, home_out, home_lse)
    attended = lax.all_to_all(attended, "tp", split_axis=0, concat_axis=0, tiled=True)
    return jnp.swapaxes(attended.reshape(heads, per_source, rows, dim), 0, 1)


def solution(mesh):
    return jax.shard_map(
        shards,
        mesh=mesh,
        in_specs=(
            P(("lend", "tp"), None, None, None),
            P(("lend", "tp"), None, None, None),
            P(("lend", "tp"), None, None, None),
            P("lend", None, "tp", None),
            P("lend", None, "tp", None),
            P("lend", None, "tp", None),
            P("lend", None, "tp", None),
            P(),
            P(),
        ),
        out_specs=P(("lend", "tp"), None, None, None),
        check_vma=False,
    )
```

```python
import math

import jax
import jax.numpy as jnp
from jax import lax
from jax.experimental import pallas as pl
from jax.experimental.pallas import tpu as pltpu
from jax.sharding import PartitionSpec as P

STEPS = 4
CAP = 2
HOME_CAP = 512
BLOCK = 512
STAT_ROWS = 8
LANES = 128
LENT_GROUP = 16
HOME_GROUP = 2
MERGE_GROUP = 4
LENT_MIB = 58

NEG_BIG = -1e30
FAR = 1 << 30
LOG2E = math.log2(math.e)

VMEM = pltpu.VMEM
SMEM = pltpu.SMEM
HBM = pltpu.HBM


def spec(space):
    return pl.BlockSpec(memory_space=space)


def nt_dot(left, right):
    return lax.dot_general(
        left, right, (((1,), (1,)), ((), ())), preferred_element_type=jnp.float32
    )


def nn_dot(left, right):
    return lax.dot_general(
        left, right, (((1,), (0,)), ((), ())), preferred_element_type=jnp.float32
    )


def pack_kernel(queries, new_keys, new_values, out, news, sems):
    per_source, heads, rows, _ = queries.shape
    fresh = [
        pltpu.make_async_copy(new_keys, news.at[0], sems.at[0]),
        pltpu.make_async_copy(new_values, news.at[1], sems.at[1]),
    ]
    copies = [
        pltpu.make_async_copy(
            queries.at[part], out.at[:, part * rows : (part + 1) * rows], sems.at[2 + part]
        )
        for part in range(per_source)
    ]
    for copy in fresh + copies:
        copy.start()
    for copy in fresh:
        copy.wait()
    fresh = [news[kind].astype(jnp.float32) for kind in range(2)]
    for head in range(heads):
        starts = [(part * heads + head) * STEPS for part in range(per_source)]
        block = [array[start : start + STEPS] for array in fresh for start in starts]
        block = jnp.concatenate(block, axis=0)
        out[head, per_source * rows :, :] = block.astype(jnp.bfloat16)
    for copy in copies:
        copy.wait()


def pick_kernel(starts, packed_ref, out_hbm, picked, sems, *, rows):
    lenders = picked.shape[0]
    parts = sems.shape[0]
    size = lenders // parts
    copies = []
    for part in range(parts):
        for place in range(part * size * CAP, (part + 1) * size * CAP):
            lender, rank = divmod(place, CAP)
            start = pl.multiple_of(starts[place], 16)
            picked[lender, rank * rows : (rank + 1) * rows, :] = packed_ref[pl.ds(start, rows), :]
        span = slice(part * size, (part + 1) * size)
        copies.append(pltpu.make_async_copy(picked.at[span], out_hbm.at[span], sems.at[part]))
        copies[-1].start()
    for copy in copies:
        copy.wait()


def home_kernel(
    info, packed_ref, keys, values, tables, asked, out_ref, lse_ref, stats, *, rows, per_source
):
    sources = packed_ref.shape[0]
    requests = sources * per_source
    new_start = rows * per_source
    new_half = STEPS * per_source
    factor = 1.0 / math.sqrt(packed_ref.shape[-1])

    stats[...] = jnp.zeros_like(stats)
    token = lax.broadcasted_iota(jnp.int32, (rows, new_half), 1)
    step = lax.broadcasted_iota(jnp.int32, (rows, new_half), 0) // (rows // STEPS)
    lane = lax.broadcasted_iota(jnp.int32, stats.shape, 1)

    def some(group, carry):
        chosen = [
            (group * HOME_GROUP + near, part)
            for near in range(HOME_GROUP)
            for part in range(per_source)
        ]
        scores, new_scores, mixed, total = [], [], [], []
        news = []
        for source, part in chosen:
            request = source * per_source + part
            query = packed_ref[source, part * rows : (part + 1) * rows, :]
            block = packed_ref[source, new_start : new_start + 2 * new_half, :].astype(jnp.float32)
            new_keys = block[:new_half].astype(jnp.bfloat16)
            news.append(block[new_half:].astype(jnp.bfloat16))
            length = jnp.minimum(info[request], HOME_CAP)
            raw = nt_dot(query, keys[request])
            position = lax.broadcasted_iota(jnp.int32, raw.shape, 1)
            scores.append(jnp.where(position < length, raw, NEG_BIG))
            seen = (token >= part * STEPS) & (token - part * STEPS <= step)
            seen = seen & (token < (part + 1) * STEPS)
            new_scores.append(jnp.where(seen, nt_dot(query, new_keys), NEG_BIG))
        tops = [
            jnp.maximum(jnp.max(old, axis=1, keepdims=True), jnp.max(new, axis=1, keepdims=True))
            for old, new in zip(scores, new_scores)
        ]
        for near, (source, part) in enumerate(chosen):
            terms = jnp.exp2((scores[near] - tops[near]) * (factor * LOG2E))
            new_terms = jnp.exp2((new_scores[near] - tops[near]) * (factor * LOG2E))
            total.append(
                jnp.sum(terms, axis=1, keepdims=True) + jnp.sum(new_terms, axis=1, keepdims=True)
            )
            mixed.append(
                nn_dot(terms.astype(jnp.bfloat16), values[source * per_source + part])
                + nn_dot(new_terms.astype(jnp.bfloat16), news[near])
            )
        collected = stats[...]
        for near, (source, part) in enumerate(chosen):
            request = source * per_source + part
            out_ref[request] = mixed[near] * (1.0 / total[near])
            collected = jnp.where(
                lane == request, tops[near] * factor + jnp.log(total[near]), collected
            )
        stats[...] = collected
        return carry

    lax.fori_loop(0, sources // HOME_GROUP, some, 0)
    turned = stats[...].T[:requests]
    lse_ref[...] = jnp.concatenate([turned] * CAP, axis=1)


def lent_kernel(
    info,
    query_hbm,
    keys_hbm,
    values_hbm,
    home_lse,
    out_ref,
    queries,
    keys,
    values,
    stats,
    sems,
    *,
    rows,
):
    slots = keys_hbm.shape[0]
    homes = query_hbm.shape[0]
    group = min(LENT_GROUP, slots)
    chunks = slots // group
    factor = 1.0 / math.sqrt(query_hbm.shape[-1])

    def copy(kind, chunk):
        source, target = ((keys_hbm, keys), (values_hbm, values))[kind]
        part = pl.ds(chunk * group, group)
        return pltpu.make_async_copy(source.at[part], target.at[part], sems.at[chunk, kind])

    arrival = pltpu.make_async_copy(query_hbm, queries, sems.at[chunks, 0])
    arrival.start()
    for chunk in range(chunks):
        for kind in range(2):
            copy(kind, chunk).start()
    stats[...] = jnp.zeros_like(stats)
    lane = lax.broadcasted_iota(jnp.int32, (rows, stats.shape[1]), 1)
    position = lax.broadcasted_iota(jnp.int32, (1, BLOCK), 1)
    arrival.wait()

    def some(chunk, carry):
        copy(0, chunk).wait()
        scores, placed, mixed, total = [], [], [], []
        for near in range(group):
            slot = chunk * group + near
            place = info[slot]
            length = info[slots + slot]
            home = lax.div(place, CAP)
            first = pl.multiple_of(lax.rem(place, CAP) * rows, rows)
            raw = nt_dot(queries[home, pl.ds(first, rows), :], keys[slot])
            scores.append(raw + jnp.where(position < length, 0.0, NEG_BIG))
            placed.append((home, first))
        tops = [jnp.max(old, axis=1, keepdims=True) for old in scores]
        copy(1, chunk).wait()
        for near in range(group):
            terms = jnp.exp2((scores[near] - tops[near]) * (factor * LOG2E))
            total.append(jnp.sum(terms, axis=1, keepdims=True))
            mixed.append(nn_dot(terms.astype(jnp.bfloat16), values[chunk * group + near]))
        for near, (home, first) in enumerate(placed):
            out_ref[home, pl.ds(first, rows), :] = (mixed[near] * (1.0 / total[near])).astype(
                jnp.bfloat16
            )
            stats[pl.ds(first, rows), :] = jnp.where(
                lane == home,
                tops[near] * factor + jnp.log(total[near]),
                stats[pl.ds(first, rows), :],
            )
        return carry

    lax.fori_loop(0, chunks, some, 0)
    turned = stats[...].T[:homes]
    high = turned.astype(jnp.bfloat16).astype(jnp.float32)
    middle = (turned - high).astype(jnp.bfloat16).astype(jnp.float32)
    low = turned - high - middle
    shape = (homes, STAT_ROWS, CAP * rows)
    row = lax.broadcasted_iota(jnp.int32, shape, 1)
    packed = jnp.where(
        row == 0,
        high[:, None, :],
        jnp.where(row == 1, middle[:, None, :], jnp.where(row == 2, low[:, None, :], 0.0)),
    )
    out_ref[:, CAP * rows :, :] = packed.astype(jnp.bfloat16)


def combine_kernel(
    info_hbm, picks_wide, back_ref, home_out, home_lse, out_ref, info, mixed, wide, sem, *, rows
):
    lenders = back_ref.shape[0]
    requests = home_out.shape[0]
    count = out_ref.shape[0]
    per_target = requests // count
    arrival = pltpu.make_async_copy(info_hbm, info, sem)
    arrival.start()

    lse = jnp.sum(back_ref[:, CAP * rows :, :].astype(jnp.float32), axis=1)
    owner = picks_wide[...]
    belongs = [owner == request for request in range(requests)]

    def per_request(values, reduce, other):
        parts = [
            reduce(jnp.where(mask, values, other), axis=0, keepdims=True) for mask in belongs
        ]
        return jnp.concatenate(parts, axis=0)

    def per_place(values, other):
        result = jnp.full(owner.shape, other, jnp.float32)
        for request, mask in enumerate(belongs):
            result = jnp.where(mask, values[request : request + 1], result)
        return result

    local = home_lse[...]
    tops = per_request(lse, jnp.max, NEG_BIG)
    tops = jnp.maximum(jnp.maximum(tops, pltpu.roll(tops, rows, 1)), local)
    weights = jnp.where(owner >= 0, jnp.exp(lse - per_place(tops, 0.0)), 0.0)
    sums = per_request(weights, jnp.sum, 0.0)
    home_weights = jnp.exp(local - tops)
    inverse = 1.0 / (home_weights + sums + pltpu.roll(sums, rows, 1))
    weights = weights * per_place(inverse, 1.0)
    home_weights = home_weights * inverse
    turned = weights.T
    for lender in range(lenders):
        wide[lender] = jnp.broadcast_to(turned[:, lender : lender + 1], wide.shape[1:])
    home_turned = home_weights.T

    for request in range(requests):
        mixed[request] = home_out[request] * home_turned[:rows, request : request + 1]
    arrival.wait()
    filled = info[0]
    places = lenders * CAP

    def some(step, carry):
        terms = []
        for near in range(MERGE_GROUP):
            entry = step * MERGE_GROUP + near
            index = jnp.minimum(entry, filled - 1)
            place = info[1 + index]
            lender = lax.div(place, CAP)
            part = pl.ds(pl.multiple_of(lax.rem(place, CAP) * rows, rows), rows)
            term = wide[lender, part, :] * back_ref[lender, part, :].astype(jnp.float32)
            terms.append((info[1 + places + index], jnp.where(entry < filled, term, 0.0)))
        for request, term in terms:
            mixed[request] = mixed[request] + term
        return carry

    lax.fori_loop(0, lax.div(filled + MERGE_GROUP - 1, MERGE_GROUP), some, 0)
    for target in range(count):
        for part in range(per_target):
            out_ref[target, part * rows : (part + 1) * rows, :] = mixed[
                target * per_target + part
            ].astype(jnp.bfloat16)


def padded(table):
    return jnp.pad(table, (0, -table.shape[0] % LANES))


def listed(present, columns):
    count = present.shape[0]
    index = jnp.arange(count, dtype=jnp.int32)
    before = index[None, :] < index[:, None]
    position = jnp.sum(present[None, :] & before, axis=1, dtype=jnp.int32)
    chosen = present[None, :] & (position[None, :] == index[:, None])
    parts = [jnp.sum(present, dtype=jnp.int32).reshape(1)]
    parts += [jnp.sum(jnp.where(chosen, column[None, :], 0), axis=1) for column in columns]
    return jnp.concatenate(parts)


def shards(
    queries,
    new_keys,
    new_values,
    home_keys,
    home_values,
    lent_keys,
    lent_values,
    lengths,
    slot_owner,
):
    tp_count = lax.axis_size("tp")
    lend_count = lax.axis_size("lend")
    me = lax.axis_index("lend").astype(jnp.int32)
    per_source, heads, rows, dim = queries.shape
    requests = per_source * tp_count
    slots = lent_keys.shape[0]
    packed_rows = per_source * (rows + 2 * STEPS)

    def params(mib):
        return pltpu.CompilerParams(vmem_limit_bytes=mib << 20)

    packed = pl.pallas_call(
        pack_kernel,
        out_shape=jax.ShapeDtypeStruct((heads, packed_rows, dim), jnp.bfloat16),
        in_specs=[spec(HBM)] * 3,
        out_specs=spec(VMEM),
        scratch_shapes=[
            pltpu.VMEM((2, per_source * heads * STEPS, dim), jnp.bfloat16),
            pltpu.SemaphoreType.DMA((2 + per_source,)),
        ],
        compiler_params=params(60),
        name="pack",
    )(queries, new_keys.reshape(-1, dim), new_values.reshape(-1, dim))
    packed = lax.all_to_all(packed, "tp", split_axis=0, concat_axis=0, tiled=True)

    table = slot_owner.reshape(lend_count, slots)
    local = table - me * requests
    code = jnp.where(
        (local >= 0) & (local < requests),
        jnp.arange(slots, dtype=jnp.int32)[None, :] * requests + local,
        FAR,
    )
    first = jnp.min(code, axis=1)
    second = jnp.min(jnp.where(code > first[:, None], code, FAR), axis=1)
    codes = jnp.stack([first, second], axis=1)
    picks_pair = jnp.where(codes < FAR, codes % requests, -1)
    picks = picks_pair.reshape(-1)
    picks_wide = jnp.repeat(picks_pair, rows, axis=1)

    own = lax.dynamic_slice_in_dim(slot_owner, me * slots, slots)
    slot = jnp.arange(slots, dtype=jnp.int32)
    everywhere = jnp.arange(slot_owner.shape[0], dtype=jnp.int32)
    same = slot_owner[None, :] == own[:, None]
    earlier = everywhere[None, :] < (me * slots + slot)[:, None]
    numbers = jnp.sum(same & earlier, axis=1, dtype=jnp.int32)
    request = jnp.arange(lengths.shape[0], dtype=jnp.int32)
    owner_length = jnp.sum(
        jnp.where(request[None, :] == own[:, None], lengths[None, :], 0), axis=1
    )
    length = owner_length - HOME_CAP - numbers * BLOCK
    home = jnp.where(own >= 0, own // requests, -1)
    before = slot[None, :] < slot[:, None]
    rank = jnp.sum((home[None, :] == home[:, None]) & before, axis=1, dtype=jnp.int32)
    place = jnp.where(own >= 0, home * CAP + rank, me * CAP)
    lent_info = jnp.concatenate([place, jnp.where(own >= 0, length, 0)])
    place_info = padded(
        listed(picks >= 0, [jnp.arange(lend_count * CAP, dtype=jnp.int32), picks])
    )
    home_lengths = lax.dynamic_slice_in_dim(lengths, me * requests, requests)

    starts = jnp.maximum(picks, 0)
    starts = (starts // per_source) * packed_rows + (starts % per_source) * rows
    asked = pl.pallas_call(
        lambda *refs: pick_kernel(*refs, rows=rows),
        out_shape=jax.ShapeDtypeStruct((lend_count, CAP * rows, dim), jnp.bfloat16),
        in_specs=[spec(SMEM), spec(VMEM)],
        out_specs=spec(HBM),
        scratch_shapes=[
            pltpu.VMEM((lend_count, CAP * rows, dim), jnp.bfloat16),
            pltpu.SemaphoreType.DMA((4,)),
        ],
        compiler_params=params(8),
        name="pick",
    )(starts, packed.reshape(tp_count * packed_rows, dim))
    arrived = lax.all_to_all(asked, "lend", split_axis=0, concat_axis=0, tiled=True)

    home_out, home_lse = pl.pallas_call(
        lambda *refs: home_kernel(*refs, rows=rows, per_source=per_source),
        out_shape=[
            jax.ShapeDtypeStruct((requests, rows, dim), jnp.float32),
            jax.ShapeDtypeStruct((requests, CAP * rows), jnp.float32),
        ],
        in_specs=[spec(SMEM)] + [spec(VMEM)] * 4 + [spec(HBM)],
        out_specs=[spec(VMEM)] * 2,
        scratch_shapes=[pltpu.VMEM((rows, LANES), jnp.float32)],
        compiler_params=params(24),
        cost_estimate=pl.CostEstimate(
            flops=4 * requests * rows * HOME_CAP * dim,
            bytes_accessed=6 << 20,
            transcendentals=requests * rows * HOME_CAP,
        ),
        name="home",
    )(
        home_lengths,
        packed,
        home_keys.reshape(requests, HOME_CAP, dim),
        home_values.reshape(requests, HOME_CAP, dim),
        picks_wide,
        asked,
    )

    back_shape = (lend_count, CAP * rows + STAT_ROWS, dim)
    back = pl.pallas_call(
        lambda *refs: lent_kernel(*refs, rows=rows),
        out_shape=jax.ShapeDtypeStruct(back_shape, jnp.bfloat16),
        in_specs=[spec(SMEM)] + [spec(HBM)] * 4,
        out_specs=spec(VMEM),
        scratch_shapes=[
            pltpu.VMEM((lend_count, CAP * rows, dim), jnp.bfloat16),
            pltpu.VMEM((slots, BLOCK, dim), jnp.bfloat16),
            pltpu.VMEM((slots, BLOCK, dim), jnp.bfloat16),
            pltpu.VMEM((CAP * rows, LANES), jnp.float32),
            pltpu.SemaphoreType.DMA((max(slots // LENT_GROUP, 1) + 1, 2)),
        ],
        compiler_params=params(LENT_MIB),
        name="lent",
    )(
        lent_info,
        arrived,
        lent_keys.reshape(slots, BLOCK, dim),
        lent_values.reshape(slots, BLOCK, dim),
        home_lse,
    )
    back = lax.all_to_all(back, "lend", split_axis=0, concat_axis=0, tiled=True)

    attended = pl.pallas_call(
        lambda *refs: combine_kernel(*refs, rows=rows),
        out_shape=jax.ShapeDtypeStruct((tp_count, per_source * rows, dim), jnp.bfloat16),
        in_specs=[spec(HBM)] + [spec(VMEM)] * 4,
        out_specs=spec(VMEM),
        scratch_shapes=[
            pltpu.SMEM(place_info.shape, jnp.int32),
            pltpu.VMEM((requests, rows, dim), jnp.float32),
            pltpu.VMEM((lend_count, CAP * rows, LANES), jnp.float32),
            pltpu.SemaphoreType.DMA,
        ],
        compiler_params=params(12),
        name="combine",
    )(place_info, picks_wide, back, home_out, home_lse)
    attended = lax.all_to_all(attended, "tp", split_axis=0, concat_axis=0, tiled=True)
    return jnp.swapaxes(attended.reshape(heads, per_source, rows, dim), 0, 1)


def solution(mesh):
    return jax.shard_map(
        shards,
        mesh=mesh,
        in_specs=(
            P(("lend", "tp"), None, None, None),
            P(("lend", "tp"), None, None, None),
            P(("lend", "tp"), None, None, None),
            P("lend", None, "tp", None),
            P("lend", None, "tp", None),
            P("lend", None, "tp", None),
            P("lend", None, "tp", None),
            P(),
            P(),
        ),
        out_specs=P(("lend", "tp"), None, None, None),
        check_vma=False,
    )
```

```python
import math

import jax
import jax.numpy as jnp
from jax import lax
from jax.experimental import pallas as pl
from jax.experimental.pallas import tpu as pltpu
from jax.sharding import PartitionSpec as P

STEPS = 4
CAP = 2
HOME_CAP = 512
BLOCK = 512
STAT_ROWS = 8
LANES = 128
LENT_GROUP = 16
HOME_GROUP = 2
MERGE_GROUP = 8
LENT_MIB = 58

NEG_BIG = -1e30
FAR = 1 << 30
LOG2E = math.log2(math.e)

VMEM = pltpu.VMEM
SMEM = pltpu.SMEM
HBM = pltpu.HBM


def spec(space):
    return pl.BlockSpec(memory_space=space)


def nt_dot(left, right):
    return lax.dot_general(
        left, right, (((1,), (1,)), ((), ())), preferred_element_type=jnp.float32
    )


def nn_dot(left, right):
    return lax.dot_general(
        left, right, (((1,), (0,)), ((), ())), preferred_element_type=jnp.float32
    )


def pack_kernel(queries, new_keys, new_values, out, news, sems):
    per_source, heads, rows, _ = queries.shape
    fresh = [
        pltpu.make_async_copy(new_keys, news.at[0], sems.at[0]),
        pltpu.make_async_copy(new_values, news.at[1], sems.at[1]),
    ]
    copies = [
        pltpu.make_async_copy(
            queries.at[part], out.at[:, part * rows : (part + 1) * rows], sems.at[2 + part]
        )
        for part in range(per_source)
    ]
    for copy in fresh + copies:
        copy.start()
    for copy in fresh:
        copy.wait()
    fresh = [news[kind].astype(jnp.float32) for kind in range(2)]
    for head in range(heads):
        starts = [(part * heads + head) * STEPS for part in range(per_source)]
        block = [array[start : start + STEPS] for array in fresh for start in starts]
        block = jnp.concatenate(block, axis=0)
        out[head, per_source * rows :, :] = block.astype(jnp.bfloat16)
    for copy in copies:
        copy.wait()


def pick_kernel(starts, packed_ref, out_hbm, picked, sems, *, rows):
    lenders = picked.shape[0]
    parts = sems.shape[0]
    size = lenders // parts
    copies = []
    for part in range(parts):
        for place in range(part * size * CAP, (part + 1) * size * CAP):
            lender, rank = divmod(place, CAP)
            start = pl.multiple_of(starts[place], 16)
            picked[lender, rank * rows : (rank + 1) * rows, :] = packed_ref[pl.ds(start, rows), :]
        span = slice(part * size, (part + 1) * size)
        copies.append(pltpu.make_async_copy(picked.at[span], out_hbm.at[span], sems.at[part]))
        copies[-1].start()
    for copy in copies:
        copy.wait()


def home_kernel(
    info, packed_ref, keys, values, tables, asked, out_ref, lse_ref, stats, *, rows, per_source
):
    sources = packed_ref.shape[0]
    requests = sources * per_source
    new_start = rows * per_source
    new_half = STEPS * per_source
    factor = 1.0 / math.sqrt(packed_ref.shape[-1])

    stats[...] = jnp.zeros_like(stats)
    token = lax.broadcasted_iota(jnp.int32, (rows, new_half), 1)
    step = lax.broadcasted_iota(jnp.int32, (rows, new_half), 0) // (rows // STEPS)
    lane = lax.broadcasted_iota(jnp.int32, stats.shape, 1)

    def some(group, carry):
        chosen = [
            (group * HOME_GROUP + near, part)
            for near in range(HOME_GROUP)
            for part in range(per_source)
        ]
        scores, new_scores, mixed, total = [], [], [], []
        news = []
        for source, part in chosen:
            request = source * per_source + part
            query = packed_ref[source, part * rows : (part + 1) * rows, :]
            block = packed_ref[source, new_start : new_start + 2 * new_half, :].astype(jnp.float32)
            new_keys = block[:new_half].astype(jnp.bfloat16)
            news.append(block[new_half:].astype(jnp.bfloat16))
            length = jnp.minimum(info[request], HOME_CAP)
            raw = nt_dot(query, keys[request])
            position = lax.broadcasted_iota(jnp.int32, raw.shape, 1)
            scores.append(jnp.where(position < length, raw, NEG_BIG))
            seen = (token >= part * STEPS) & (token - part * STEPS <= step)
            seen = seen & (token < (part + 1) * STEPS)
            new_scores.append(jnp.where(seen, nt_dot(query, new_keys), NEG_BIG))
        tops = [
            jnp.maximum(jnp.max(old, axis=1, keepdims=True), jnp.max(new, axis=1, keepdims=True))
            for old, new in zip(scores, new_scores)
        ]
        for near, (source, part) in enumerate(chosen):
            terms = jnp.exp2((scores[near] - tops[near]) * (factor * LOG2E))
            new_terms = jnp.exp2((new_scores[near] - tops[near]) * (factor * LOG2E))
            total.append(
                jnp.sum(terms, axis=1, keepdims=True) + jnp.sum(new_terms, axis=1, keepdims=True)
            )
            mixed.append(
                nn_dot(terms.astype(jnp.bfloat16), values[source * per_source + part])
                + nn_dot(new_terms.astype(jnp.bfloat16), news[near])
            )
        collected = stats[...]
        for near, (source, part) in enumerate(chosen):
            request = source * per_source + part
            out_ref[request] = mixed[near] * (1.0 / total[near])
            collected = jnp.where(
                lane == request, tops[near] * factor + jnp.log(total[near]), collected
            )
        stats[...] = collected
        return carry

    lax.fori_loop(0, sources // HOME_GROUP, some, 0)
    turned = stats[...].T[:requests]
    lse_ref[...] = jnp.concatenate([turned] * CAP, axis=1)


def lent_kernel(
    info,
    query_hbm,
    keys_hbm,
    values_hbm,
    home_lse,
    out_ref,
    queries,
    keys,
    values,
    stats,
    sems,
    *,
    rows,
):
    slots = keys_hbm.shape[0]
    homes = query_hbm.shape[0]
    group = min(LENT_GROUP, slots)
    chunks = slots // group
    factor = 1.0 / math.sqrt(query_hbm.shape[-1])

    def copy(kind, chunk):
        source, target = ((keys_hbm, keys), (values_hbm, values))[kind]
        part = pl.ds(chunk * group, group)
        return pltpu.make_async_copy(source.at[part], target.at[part], sems.at[chunk, kind])

    arrival = pltpu.make_async_copy(query_hbm, queries, sems.at[chunks, 0])
    arrival.start()
    for chunk in range(chunks):
        for kind in range(2):
            copy(kind, chunk).start()
    stats[...] = jnp.zeros_like(stats)
    lane = lax.broadcasted_iota(jnp.int32, (rows, stats.shape[1]), 1)
    position = lax.broadcasted_iota(jnp.int32, (1, BLOCK), 1)
    arrival.wait()

    def some(chunk, carry):
        copy(0, chunk).wait()
        scores, placed, mixed, total = [], [], [], []
        for near in range(group):
            slot = chunk * group + near
            place = info[slot]
            length = info[slots + slot]
            home = lax.div(place, CAP)
            first = pl.multiple_of(lax.rem(place, CAP) * rows, rows)
            raw = nt_dot(queries[home, pl.ds(first, rows), :], keys[slot])
            scores.append(raw + jnp.where(position < length, 0.0, NEG_BIG))
            placed.append((home, first))
        tops = [jnp.max(old, axis=1, keepdims=True) for old in scores]
        copy(1, chunk).wait()
        for near in range(group):
            terms = jnp.exp2((scores[near] - tops[near]) * (factor * LOG2E))
            total.append(jnp.sum(terms, axis=1, keepdims=True))
            mixed.append(nn_dot(terms.astype(jnp.bfloat16), values[chunk * group + near]))
        for near, (home, first) in enumerate(placed):
            out_ref[home, pl.ds(first, rows), :] = (mixed[near] * (1.0 / total[near])).astype(
                jnp.bfloat16
            )
            stats[pl.ds(first, rows), :] = jnp.where(
                lane == home,
                tops[near] * factor + jnp.log(total[near]),
                stats[pl.ds(first, rows), :],
            )
        return carry

    lax.fori_loop(0, chunks, some, 0)
    turned = stats[...].T[:homes]
    high = turned.astype(jnp.bfloat16).astype(jnp.float32)
    middle = (turned - high).astype(jnp.bfloat16).astype(jnp.float32)
    low = turned - high - middle
    shape = (homes, STAT_ROWS, CAP * rows)
    row = lax.broadcasted_iota(jnp.int32, shape, 1)
    packed = jnp.where(
        row == 0,
        high[:, None, :],
        jnp.where(row == 1, middle[:, None, :], jnp.where(row == 2, low[:, None, :], 0.0)),
    )
    out_ref[:, CAP * rows :, :] = packed.astype(jnp.bfloat16)


def combine_kernel(
    info_hbm, picks_wide, back_ref, home_out, home_lse, out_ref, info, mixed, wide, sem, *, rows
):
    lenders = back_ref.shape[0]
    requests = home_out.shape[0]
    count = out_ref.shape[0]
    per_target = requests // count
    arrival = pltpu.make_async_copy(info_hbm, info, sem)
    arrival.start()

    lse = jnp.sum(back_ref[:, CAP * rows :, :].astype(jnp.float32), axis=1)
    owner = picks_wide[...]
    belongs = [owner == request for request in range(requests)]

    def per_request(values, reduce, other):
        parts = [
            reduce(jnp.where(mask, values, other), axis=0, keepdims=True) for mask in belongs
        ]
        return jnp.concatenate(parts, axis=0)

    def per_place(values, other):
        result = jnp.full(owner.shape, other, jnp.float32)
        for request, mask in enumerate(belongs):
            result = jnp.where(mask, values[request : request + 1], result)
        return result

    local = home_lse[...]
    tops = per_request(lse, jnp.max, NEG_BIG)
    tops = jnp.maximum(jnp.maximum(tops, pltpu.roll(tops, rows, 1)), local)
    weights = jnp.where(owner >= 0, jnp.exp(lse - per_place(tops, 0.0)), 0.0)
    sums = per_request(weights, jnp.sum, 0.0)
    home_weights = jnp.exp(local - tops)
    inverse = 1.0 / (home_weights + sums + pltpu.roll(sums, rows, 1))
    weights = weights * per_place(inverse, 1.0)
    home_weights = home_weights * inverse
    turned = weights.T
    for lender in range(lenders):
        wide[lender] = jnp.broadcast_to(turned[:, lender : lender + 1], wide.shape[1:])
    home_turned = home_weights.T

    for request in range(requests):
        mixed[request] = home_out[request] * home_turned[:rows, request : request + 1]
    arrival.wait()
    filled = info[0]
    places = lenders * CAP

    def some(step, carry):
        terms = []
        for near in range(MERGE_GROUP):
            entry = step * MERGE_GROUP + near
            index = jnp.minimum(entry, filled - 1)
            place = info[1 + index]
            lender = lax.div(place, CAP)
            part = pl.ds(pl.multiple_of(lax.rem(place, CAP) * rows, rows), rows)
            term = wide[lender, part, :] * back_ref[lender, part, :].astype(jnp.float32)
            terms.append((info[1 + places + index], jnp.where(entry < filled, term, 0.0)))
        for request, term in terms:
            mixed[request] = mixed[request] + term
        return carry

    lax.fori_loop(0, lax.div(filled + MERGE_GROUP - 1, MERGE_GROUP), some, 0)
    for target in range(count):
        for part in range(per_target):
            out_ref[target, part * rows : (part + 1) * rows, :] = mixed[
                target * per_target + part
            ].astype(jnp.bfloat16)


def padded(table):
    return jnp.pad(table, (0, -table.shape[0] % LANES))


def listed(present, columns):
    count = present.shape[0]
    index = jnp.arange(count, dtype=jnp.int32)
    before = index[None, :] < index[:, None]
    position = jnp.sum(present[None, :] & before, axis=1, dtype=jnp.int32)
    chosen = present[None, :] & (position[None, :] == index[:, None])
    parts = [jnp.sum(present, dtype=jnp.int32).reshape(1)]
    parts += [jnp.sum(jnp.where(chosen, column[None, :], 0), axis=1) for column in columns]
    return jnp.concatenate(parts)


def shards(
    queries,
    new_keys,
    new_values,
    home_keys,
    home_values,
    lent_keys,
    lent_values,
    lengths,
    slot_owner,
):
    tp_count = lax.axis_size("tp")
    lend_count = lax.axis_size("lend")
    me = lax.axis_index("lend").astype(jnp.int32)
    per_source, heads, rows, dim = queries.shape
    requests = per_source * tp_count
    slots = lent_keys.shape[0]
    packed_rows = per_source * (rows + 2 * STEPS)

    def params(mib):
        return pltpu.CompilerParams(vmem_limit_bytes=mib << 20)

    packed = pl.pallas_call(
        pack_kernel,
        out_shape=jax.ShapeDtypeStruct((heads, packed_rows, dim), jnp.bfloat16),
        in_specs=[spec(HBM)] * 3,
        out_specs=spec(VMEM),
        scratch_shapes=[
            pltpu.VMEM((2, per_source * heads * STEPS, dim), jnp.bfloat16),
            pltpu.SemaphoreType.DMA((2 + per_source,)),
        ],
        compiler_params=params(60),
        name="pack",
    )(queries, new_keys.reshape(-1, dim), new_values.reshape(-1, dim))
    packed = lax.all_to_all(packed, "tp", split_axis=0, concat_axis=0, tiled=True)

    table = slot_owner.reshape(lend_count, slots)
    local = table - me * requests
    code = jnp.where(
        (local >= 0) & (local < requests),
        jnp.arange(slots, dtype=jnp.int32)[None, :] * requests + local,
        FAR,
    )
    first = jnp.min(code, axis=1)
    second = jnp.min(jnp.where(code > first[:, None], code, FAR), axis=1)
    codes = jnp.stack([first, second], axis=1)
    picks_pair = jnp.where(codes < FAR, codes % requests, -1)
    picks = picks_pair.reshape(-1)
    picks_wide = jnp.repeat(picks_pair, rows, axis=1)

    own = lax.dynamic_slice_in_dim(slot_owner, me * slots, slots)
    slot = jnp.arange(slots, dtype=jnp.int32)
    everywhere = jnp.arange(slot_owner.shape[0], dtype=jnp.int32)
    same = slot_owner[None, :] == own[:, None]
    earlier = everywhere[None, :] < (me * slots + slot)[:, None]
    numbers = jnp.sum(same & earlier, axis=1, dtype=jnp.int32)
    request = jnp.arange(lengths.shape[0], dtype=jnp.int32)
    owner_length = jnp.sum(
        jnp.where(request[None, :] == own[:, None], lengths[None, :], 0), axis=1
    )
    length = owner_length - HOME_CAP - numbers * BLOCK
    home = jnp.where(own >= 0, own // requests, -1)
    before = slot[None, :] < slot[:, None]
    rank = jnp.sum((home[None, :] == home[:, None]) & before, axis=1, dtype=jnp.int32)
    place = jnp.where(own >= 0, home * CAP + rank, me * CAP)
    lent_info = jnp.concatenate([place, jnp.where(own >= 0, length, 0)])
    place_info = padded(
        listed(picks >= 0, [jnp.arange(lend_count * CAP, dtype=jnp.int32), picks])
    )
    home_lengths = lax.dynamic_slice_in_dim(lengths, me * requests, requests)

    starts = jnp.maximum(picks, 0)
    starts = (starts // per_source) * packed_rows + (starts % per_source) * rows
    asked = pl.pallas_call(
        lambda *refs: pick_kernel(*refs, rows=rows),
        out_shape=jax.ShapeDtypeStruct((lend_count, CAP * rows, dim), jnp.bfloat16),
        in_specs=[spec(SMEM), spec(VMEM)],
        out_specs=spec(HBM),
        scratch_shapes=[
            pltpu.VMEM((lend_count, CAP * rows, dim), jnp.bfloat16),
            pltpu.SemaphoreType.DMA((4,)),
        ],
        compiler_params=params(8),
        name="pick",
    )(starts, packed.reshape(tp_count * packed_rows, dim))
    arrived = lax.all_to_all(asked, "lend", split_axis=0, concat_axis=0, tiled=True)

    home_out, home_lse = pl.pallas_call(
        lambda *refs: home_kernel(*refs, rows=rows, per_source=per_source),
        out_shape=[
            jax.ShapeDtypeStruct((requests, rows, dim), jnp.float32),
            jax.ShapeDtypeStruct((requests, CAP * rows), jnp.float32),
        ],
        in_specs=[spec(SMEM)] + [spec(VMEM)] * 4 + [spec(HBM)],
        out_specs=[spec(VMEM)] * 2,
        scratch_shapes=[pltpu.VMEM((rows, LANES), jnp.float32)],
        compiler_params=params(24),
        cost_estimate=pl.CostEstimate(
            flops=4 * requests * rows * HOME_CAP * dim,
            bytes_accessed=6 << 20,
            transcendentals=requests * rows * HOME_CAP,
        ),
        name="home",
    )(
        home_lengths,
        packed,
        home_keys.reshape(requests, HOME_CAP, dim),
        home_values.reshape(requests, HOME_CAP, dim),
        picks_wide,
        asked,
    )

    back_shape = (lend_count, CAP * rows + STAT_ROWS, dim)
    back = pl.pallas_call(
        lambda *refs: lent_kernel(*refs, rows=rows),
        out_shape=jax.ShapeDtypeStruct(back_shape, jnp.bfloat16),
        in_specs=[spec(SMEM)] + [spec(HBM)] * 4,
        out_specs=spec(VMEM),
        scratch_shapes=[
            pltpu.VMEM((lend_count, CAP * rows, dim), jnp.bfloat16),
            pltpu.VMEM((slots, BLOCK, dim), jnp.bfloat16),
            pltpu.VMEM((slots, BLOCK, dim), jnp.bfloat16),
            pltpu.VMEM((CAP * rows, LANES), jnp.float32),
            pltpu.SemaphoreType.DMA((max(slots // LENT_GROUP, 1) + 1, 2)),
        ],
        compiler_params=params(LENT_MIB),
        name="lent",
    )(
        lent_info,
        arrived,
        lent_keys.reshape(slots, BLOCK, dim),
        lent_values.reshape(slots, BLOCK, dim),
        home_lse,
    )
    back = lax.all_to_all(back, "lend", split_axis=0, concat_axis=0, tiled=True)

    attended = pl.pallas_call(
        lambda *refs: combine_kernel(*refs, rows=rows),
        out_shape=jax.ShapeDtypeStruct((tp_count, per_source * rows, dim), jnp.bfloat16),
        in_specs=[spec(HBM)] + [spec(VMEM)] * 4,
        out_specs=spec(VMEM),
        scratch_shapes=[
            pltpu.SMEM(place_info.shape, jnp.int32),
            pltpu.VMEM((requests, rows, dim), jnp.float32),
            pltpu.VMEM((lend_count, CAP * rows, LANES), jnp.float32),
            pltpu.SemaphoreType.DMA,
        ],
        compiler_params=params(12),
        name="combine",
    )(place_info, picks_wide, back, home_out, home_lse)
    attended = lax.all_to_all(attended, "tp", split_axis=0, concat_axis=0, tiled=True)
    return jnp.swapaxes(attended.reshape(heads, per_source, rows, dim), 0, 1)


def solution(mesh):
    return jax.shard_map(
        shards,
        mesh=mesh,
        in_specs=(
            P(("lend", "tp"), None, None, None),
            P(("lend", "tp"), None, None, None),
            P(("lend", "tp"), None, None, None),
            P("lend", None, "tp", None),
            P("lend", None, "tp", None),
            P("lend", None, "tp", None),
            P("lend", None, "tp", None),
            P(),
            P(),
        ),
        out_specs=P(("lend", "tp"), None, None, None),
        check_vma=False,
    )
```
